32 devices in a mesh: task: 4 (over y, x), batch: 8 (over z, core).
Axes of the slice: x: 2, y: 2, z: 4, core: 2. Of those that a mesh axis runs over, the one named last changes fastest.
Arguments:
- tokens: bfloat16 [128, 256, 1024], P(('task', 'batch')), may hold values from -6 to 6
- cotangent: bfloat16 [128, 256, 1024], P(('task', 'batch')), may hold values from -6 to 6
- task_ids: int32 [128], P(('task', 'batch')), may hold values from 0 to 15, as said below
- qkv_weight: bfloat16 [1024, 3072], P(('task', 'batch')), may hold values from -0.1875 to 0.1875
- out_weight: bfloat16 [1024, 1024], P(('task', 'batch')), may hold values from -0.75 to 0.75
- fc_weight: bfloat16 [1024, 4096], P(('task', 'batch')), may hold values from -0.1875 to 0.1875
- proj_weight: bfloat16 [4096, 1024], P(('task', 'batch')), may hold values from -0.09375 to 0.09375
- norm1_gain: float32 [1024], replicated, may hold values from 0.5 to 1.5
- norm1_shift: float32 [1024], replicated, may hold values from -1.2 to 1.2
- norm2_gain: float32 [1024], replicated, may hold values from 0.5 to 1.5
- norm2_shift: float32 [1024], replicated, may hold values from -1.2 to 1.2
- prefix_embed: bfloat16 [16, 10, 1024], P('task'), may hold values from -6 to 6
- reparam_in: bfloat16 [16, 1024, 512], P('task'), may hold values from -0.1875 to 0.1875
- reparam_in_bias: bfloat16 [16, 512], P('task'), may hold values from -3 to 3
- reparam_out: bfloat16 [16, 512, 2048], P('task'), may hold values from -0.25 to 0.25
- reparam_out_bias: bfloat16 [16, 2048], P('task'), may hold values from -3 to 3
Outputs:
- block_out: bfloat16 [128, 256, 1024], P(('task', 'batch'))
- input_grad: bfloat16 [128, 256, 1024], P(('task', 'batch'))
- embed_grad: float32 [16, 10, 1024], P('task', None, 'batch')
- reparam_in_grad: float32 [16, 1024, 512], P('task', 'batch')
- reparam_in_bias_grad: float32 [16, 512], P('task', 'batch')
- reparam_out_grad: float32 [16, 512, 2048], P('task', 'batch')
- reparam_out_bias_grad: float32 [16, 2048], P('task', 'batch')
The draws below stay inside these ranges and needn't reach their ends.
Inputs may be any that keep to these rules, and one draw needn't show every extreme that they name: `task_ids`: tasks 4 * g to 4 * g + 3 form group g, held by index g of axis task. Of the 4 examples of one device at most 2 have tasks in one group; in every draw one group, drawn anew, has exactly 2 examples of every device.
All inputs are finite; a program needn't handle non-finite values.
Results may differ from the reference program's by a relative error of at most 0.015.
Values may be sent and summed in bfloat16 or wider, within the bound.
A program may use at most 320 MiB of HBM per device.

```python
import math
import jax
import jax.numpy as jnp
from jax import lax

D = 1024
HEADS = 16
FF = 4096
R = 512
P_SIZE = 10
SEQ = 256
EX_DEV = 4
TASK_GROUP = 4
CAP = 2
EXAMPLES = 128
TASKS = 16
N_TASK = 4


def draw_task_ids(key, part):
    key = jax.random.fold_in(key, 7)
    key_list = jax.random.split(key, 6)
    device_count = EXAMPLES // EX_DEV
    hot_group = jax.random.randint(key_list[0], (), 0, N_TASK)
    offsets = jax.random.randint(key_list[1], (device_count, EX_DEV), 1, N_TASK)
    places = jnp.arange(EX_DEV)[None, :]
    groups_of = jnp.where(places < CAP, hot_group, (hot_group + offsets) % N_TASK)
    ranking = jax.random.randint(key_list[2], (device_count, EX_DEV), 0, 1 << 20) * EX_DEV + places
    ordering = jnp.argsort(ranking, axis=1)
    groups_of = jnp.take_along_axis(groups_of, ordering, axis=1)
    hot_local = jax.random.randint(key_list[3], (N_TASK,), 0, TASK_GROUP)
    coin_flip = jax.random.randint(key_list[4], (device_count, EX_DEV), 0, 2)
    free_local = jax.random.randint(key_list[5], (device_count, EX_DEV), 0, TASK_GROUP)
    local_task = jnp.where(coin_flip == 0, hot_local[groups_of], free_local)
    return (groups_of * TASK_GROUP + local_task).reshape(EXAMPLES).astype(jnp.int32)


def levels(own_key, extent, shards, smallest, top_value):
    level = 1.0
    for axis_at, shards_of in shards:
        draws = jax.random.uniform(jax.random.fold_in(jax.random.fold_in(own_key, 6), axis_at), (shards_of,), jnp.float32, smallest / len(shards), top_value / len(shards))
        level = level * jnp.repeat(jnp.exp(draws), extent[axis_at] // shards_of).reshape((-1,) + (1,) * (len(extent) - 1 - axis_at))
    return level


def noise(key, extent, scale, limit, cuts=(), dtype=jnp.bfloat16):
    drawn = jax.random.normal(key, extent, jnp.float32) * scale
    if len(cuts) > 0:
        drawn = levels(key, extent, cuts, -0.22, 0.18) * drawn
    return jnp.clip(drawn, min=-limit, max=limit).astype(dtype)


def setup_inputs(seed: int = 0) -> dict:
    key_of = jax.random.split(jax.random.key(seed), 17)
    return {
        "tokens": noise(key_of[0], (EXAMPLES, SEQ, D), 1.0, 6.0, ((0, 32),)),
        "cotangent": noise(key_of[1], (EXAMPLES, SEQ, D), 1.0, 6.0, ((0, 32),)),
        "task_ids": draw_task_ids(jax.random.fold_in(key_of[16], 71), 0),
        "qkv_weight": noise(key_of[3], (D, 3 * D), D ** -0.5, 0.1875, ((0, 32),)),
        "out_weight": noise(key_of[4], (D, D), (D // 16) ** -0.5, 0.75, ((0, 32),)),
        "fc_weight": noise(key_of[5], (D, FF), D ** -0.5, 0.1875, ((0, 32),)),
        "proj_weight": noise(key_of[6], (FF, D), FF ** -0.5, 0.09375, ((0, 32),)),
        "norm1_gain": jnp.clip(1.0 + 0.1 * jax.random.normal(key_of[7], (D,), jnp.float32), 0.5, 1.5),
        "norm1_shift": noise(key_of[8], (D,), 0.3, 1.2, (), jnp.float32),
        "norm2_gain": jnp.clip(1.0 + 0.1 * jax.random.normal(key_of[9], (D,), jnp.float32), 0.5, 1.5),
        "norm2_shift": noise(key_of[10], (D,), 0.3, 1.2, (), jnp.float32),
        "prefix_embed": noise(key_of[11], (TASKS, P_SIZE, D), 1.0, 6.0, ((0, 4),)),
        "reparam_in": noise(key_of[12], (TASKS, D, R), D ** -0.5, 0.1875, ((0, 4),)),
        "reparam_in_bias": noise(key_of[13], (TASKS, R), 0.5, 3.0, ((0, 4),)),
        "reparam_out": noise(key_of[14], (TASKS, R, 2 * D), R ** -0.5, 0.25, ((0, 4),)),
        "reparam_out_bias": noise(key_of[15], (TASKS, 2 * D), 0.5, 3.0, ((0, 4),)),
    }


highest = lax.Precision.HIGHEST
epsilon = 1e-05

@jax.custom_vjp
def low(v):
    return lax.optimization_barrier(v.astype(jnp.bfloat16)).astype(jnp.float32)

@jax.custom_vjp
def low_back(v):
    return v

def low_keep(v):
    return (low(v), None)

def low_pass(kept, grad):
    return (grad,)

def back_keep(v):
    return (v, None)

def back_low(kept, grad):
    return (low(grad),)
low.defvjp(low_keep, low_pass)
low_back.defvjp(back_keep, back_low)

def layer_norm(values_in, norm_gain, norm_shift):
    average = lax.optimization_barrier(jnp.mean(values_in, -1, keepdims=True))
    centred = values_in - average
    spread = lax.optimization_barrier(jnp.mean(centred * centred, -1, keepdims=True))
    return centred * lax.rsqrt(spread + epsilon) * norm_gain + norm_shift

def frozen_block(inputs, prefix_kv, frozen):
    w_qkv, w_out, w_fc, w_proj, gain_one, shift_one, gain_two, shift_two = frozen
    ex_count, seq_len, model_width = inputs.shape
    prefix_len = prefix_kv.shape[1]
    head_dim = model_width // HEADS
    normed = low(layer_norm(inputs, gain_one, shift_one))
    mixed_qkv = jnp.einsum('gsd,de->gse', normed, w_qkv, precision=highest)
    queries = low_back(low(mixed_qkv[..., :model_width] * head_dim ** (-0.5)))
    keys_tok = low_back(low(mixed_qkv[..., model_width:2 * model_width]))
    values_tok = low_back(low(mixed_qkv[..., 2 * model_width:]))
    all_keys = jnp.concatenate([prefix_kv[..., :model_width], keys_tok], axis=1)
    all_values = jnp.concatenate([prefix_kv[..., model_width:], values_tok], axis=1)
    all_keys = all_keys.reshape(ex_count, prefix_len + seq_len, HEADS, head_dim)
    all_values = all_values.reshape(ex_count, prefix_len + seq_len, HEADS, head_dim)
    queries = queries.reshape(ex_count, seq_len, HEADS, head_dim)
    scores = low_back(jnp.einsum('gqhe,gkhe->ghqk', queries, all_keys, precision=highest))
    rows_at = jnp.arange(seq_len)[:, None]
    cols_at = jnp.arange(prefix_len + seq_len)[None, :] - prefix_len
    scores = jnp.where(cols_at <= rows_at, scores, -1e+30)
    row_top = lax.optimization_barrier(jnp.max(scores, -1, keepdims=True))
    exps = jnp.exp(scores - row_top)
    probs = low(exps / lax.optimization_barrier(jnp.sum(exps, -1, keepdims=True)))
    attended = jnp.einsum('ghqk,gkhe->gqhe', probs, all_values, precision=highest)
    attended = low_back(low(attended.reshape(ex_count, seq_len, model_width)))
    residual = inputs + low_back(jnp.einsum('gse,ed->gsd', attended, w_out, precision=highest))
    normed_two = low(layer_norm(residual, gain_two, shift_two))
    upward = low_back(jnp.einsum('gsd,df->gsf', normed_two, w_fc, precision=highest))
    activated = low(jax.nn.gelu(upward, approximate=True))
    return residual + low_back(jnp.einsum('gsf,fd->gsd', activated, w_proj, precision=highest))

def reference(tokens, cotangent, task_ids, qkv_weight, out_weight, fc_weight, proj_weight, norm1_gain, norm1_shift, norm2_gain, norm2_shift, prefix_embed, reparam_in, reparam_in_bias, reparam_out, reparam_out_bias):
    frozen = tuple((weight_item.astype(jnp.float32) for weight_item in (qkv_weight, out_weight, fc_weight, proj_weight, norm1_gain, norm1_shift, norm2_gain, norm2_shift)))
    example_total = tokens.shape[0]
    group_size = math.gcd(example_total, max(1, 4096 // SEQ))
    group_runs = example_total // group_size

    def forward(inputs, embed, in_weight, in_bias, out_matrix, out_bias):
        pre_act = jnp.einsum('tpd,tdr->tpr', embed, in_weight, precision=highest) + in_bias[:, None, :]
        hidden = low(jnp.tanh(pre_act))
        kv_table = low(jnp.einsum('tpr,trc->tpc', hidden, out_matrix, precision=highest) + out_bias[:, None, :])
        example_kv = kv_table[task_ids]
        run_inputs = inputs.reshape(group_runs, group_size, SEQ, D)
        run_kv = example_kv.reshape(group_runs, group_size, P_SIZE, 2 * D)
        run_block = jax.checkpoint(lambda pair_in: frozen_block(pair_in[0], pair_in[1], frozen))
        outputs = lax.map(run_block, (run_inputs, run_kv))
        return outputs.reshape(inputs.shape)
    output, pullback = jax.vjp(forward, tokens.astype(jnp.float32), prefix_embed.astype(jnp.float32), reparam_in.astype(jnp.float32), reparam_in_bias.astype(jnp.float32), reparam_out.astype(jnp.float32), reparam_out_bias.astype(jnp.float32))
    grads = pullback(cotangent.astype(jnp.float32))
    return (output.astype(jnp.bfloat16), grads[0].astype(jnp.bfloat16), grads[1], grads[2], grads[3], grads[4], grads[5])
```

```python
import functools

import jax
import jax.numpy as jnp
from jax import lax
from jax.experimental import pallas as pl
from jax.experimental.pallas import tpu as pltpu
from jax.sharding import PartitionSpec as P

HEADS = 16
HEAD_DIM = 64
CAP = 2
QUADS = 4
QUAD_HEADS = HEADS // QUADS
PAD = 16
CHUNKS = 4
MASKED = -1e30
MIB = 1024 * 1024

highest = lax.Precision.HIGHEST
epsilon = 1e-05
bf16 = jnp.bfloat16
f32 = jnp.float32
NT_DIMS = (((1,), (1,)), ((), ()))


def dot_nn(left, right):
    return jnp.dot(left, right, preferred_element_type=f32)


def dot_nt(left, right):
    return lax.dot_general(left, right, NT_DIMS, preferred_element_type=f32)


def rows_of(value):
    return value.reshape(-1, value.shape[-1])


class Gather:
    def __init__(self, place, held, ssem, rsem, osem, base, owns):
        self.place, self.held = place, held
        self.ssem, self.rsem, self.osem, self.base = ssem, rsem, osem, base
        self.owns = owns
        self.line = place["line"]
        self.cut = self.line // 2

    @staticmethod
    def semaphores(line):
        return (line - 1) + 8

    def remote(self, ref, at, target):
        return pltpu.make_async_remote_copy(
            src_ref=ref,
            dst_ref=ref,
            send_sem=self.ssem.at[self.base + at],
            recv_sem=self.rsem.at[self.base + at],
            device_id=target,
            device_id_type=pl.DeviceIdType.MESH,
        )

    def own_copies(self):
        slot = self.held.at[self.place["t"], self.place["z"], self.place["c"]]
        return [
            pltpu.make_async_copy(source, slot.at[where], self.osem.at[index])
            for source, where, index in self.owns
        ]

    def to_line(self, k):
        p = self.place
        target = (p["t"], lax.rem(p["z"] + k, self.line) * 2 + p["c"])
        return self.remote(self.held.at[p["t"], p["z"], p["c"]], k - 1, target)

    def part(self, flip, first, last, at, target):
        p = self.place
        return self.remote(
            self.held.at[p["t"] ^ flip, first:last, p["c"]], self.line - 1 + at, target
        )

    NAMES = ("x", "y", "xr", "yr", "s0", "s1", "s2", "s3")

    def copy(self, name):
        p, n = self.place, self.line
        at = self.NAMES.index(name)
        if name[0] == "s":
            return self.part(int(name[1]), 0, n, at, (p["t"], p["z"] * 2 + 1 - p["c"]))
        step = 1 if name[0] == "x" else 2
        target = (p["t"] ^ step, p["z"] * 2 + p["c"])
        if name[1:] == "r":
            first, last = (0, self.cut) if step == 1 else (self.cut, n)
            return self.part(3 - step, first, last, at, target)
        return self.part(0, 0, n, at, target)

    def begin(self):
        for copy in self.own_copies():
            copy.start()

    def stage(self, step):
        c = self.copy
        if step == 0:
            for copy in self.own_copies():
                copy.wait()
            for k in range(1, self.line):
                self.to_line(k).start()
        elif step == 1:
            for k in range(1, self.line):
                self.to_line(k).wait_recv()
            c("x").start()
            c("y").start()
            c("s0").start()
        elif step == 2:
            c("x").wait_recv()
            c("yr").start()
            c("s1").start()
            c("y").wait_recv()
            c("xr").start()
            c("s2").start()
        elif step == 3:
            c("xr").wait_recv()
            c("yr").wait_recv()
            c("s3").start()
        elif step == 4:
            for name in ("s0", "s1", "s2", "s3"):
                c(name).wait_recv()

    def finish(self):
        for k in range(1, self.line):
            self.to_line(k).wait_send()
        for name in self.NAMES:
            self.copy(name).wait_send()


class GatherRows(Gather):
    def __init__(self, place, held, ssem, rsem, osem, base, owns, piece):
        super().__init__(place, held, ssem, rsem, osem, base, owns)
        self.piece = piece

    @staticmethod
    def semaphores(line):
        return (line - 1) + 8 * line

    def part(self, flip, first, last, at, target):
        p = self.place
        rows = self.held.shape[3]
        lo, hi = first * rows // self.line, last * rows // self.line
        return self.remote(
            self.held.at[p["t"] ^ flip, self.piece, p["c"], lo:hi],
            self.line - 1 + 8 * self.piece + at,
            target,
        )

    def begin(self):
        if self.piece == 0:
            super().begin()

    def stage(self, step):
        if step == 0 and self.piece > 0:
            return
        if step == 1:
            c = self.copy
            if self.piece == 0:
                for k in range(1, self.line):
                    self.to_line(k).wait_recv()
            c("x").start()
            c("y").start()
            c("s0").start()
        else:
            super().stage(step)

    def finish(self):
        if self.piece == 0:
            for k in range(1, self.line):
                self.to_line(k).wait_send()
        for name in self.NAMES:
            self.copy(name).wait_send()


class Local:
    def __init__(self, held, osem, owns):
        self.held, self.osem, self.owns = held, osem, owns

    def own_copies(self):
        return [
            pltpu.make_async_copy(source, self.held.at[where], self.osem.at[index])
            for source, where, index in self.owns
        ]

    def begin(self):
        for copy in self.own_copies():
            copy.start()

    def stage(self, step):
        if step == 4:
            for copy in self.own_copies():
                copy.wait()

    def finish(self):
        pass


class Pump:
    LAG = 4

    def __init__(self, units):
        self.units = units
        self.order = []
        for i in range(len(units) + self.LAG):
            for step in range(5):
                u = i - step
                if 0 <= u < len(units):
                    self.order.append((u, step))
        self.done = 0

    def begin(self):
        for unit in self.units:
            unit.begin()

    def run(self, count):
        for _ in range(count):
            if self.done < len(self.order):
                u, step = self.order[self.done]
                self.units[u].stage(step)
                self.done += 1

    def ready(self, unit):
        last = self.order.index((unit, 4)) + 1
        self.run(max(0, last - self.done))

    def finish(self):
        self.run(len(self.order))
        for unit in self.units:
            unit.finish()


def norm_parts(value):
    average = jnp.mean(value, -1, keepdims=True)
    centred = value - average
    spread = jnp.mean(centred * centred, -1, keepdims=True)
    inverse = lax.rsqrt(spread + epsilon)
    return centred * inverse, inverse


def norm_back(value, gain, grad):
    hat, inverse = norm_parts(value)
    scaled = grad * gain
    first = jnp.mean(scaled, -1, keepdims=True)
    second = jnp.mean(scaled * hat, -1, keepdims=True)
    return inverse * (scaled - first - hat * second)


def spread_heads(block):
    lane = lax.broadcasted_iota(jnp.int32, (1, block.shape[1]), 1) // HEAD_DIM
    return jnp.concatenate(
        [jnp.where(lane == h, block, jnp.zeros_like(block)) for h in range(QUAD_HEADS)], axis=0
    )


def join_heads(block, rows):
    lane = lax.broadcasted_iota(jnp.int32, (1, block.shape[1]), 1) // HEAD_DIM
    total = block[:rows]
    for h in range(1, QUAD_HEADS):
        total = jnp.where(lane == h, block[h * rows : (h + 1) * rows], total)
    return total


def counted_keys(seq, prefix):
    key = lax.broadcasted_iota(jnp.int32, (seq + PAD, seq), 0)
    query = lax.broadcasted_iota(jnp.int32, (seq + PAD, seq), 1)
    return jnp.where(key < seq, key, jnp.where(key < seq + prefix, 0, seq)) <= query


def block_kernel(cfg, *refs):
    it = iter(refs)
    take = lambda n: [next(it) for _ in range(n)]
    tok_in, cot_in, ids, gain1, shift1, gain2, shift2 = take(7)
    wqkv, wout, wfc, wproj, table = take(5)
    block_to, grad_to, prefix_grad = take(3)
    h_tab, h_q0, h_q1, h_q2, h_q3, h_out = take(6)
    h_fc = take(CHUNKS)
    (h_proj,) = take(1)
    tok, cot, qkv, normed, att, res, acc, gacc, pkv, lse = take(10)
    ssem, rsem, osem, isem = take(4)
    h_q = (h_q0, h_q1, h_q2, h_q3)

    seq, width, examples, prefix = cfg["seq"], cfg["width"], cfg["examples"], cfg["prefix"]
    rows, hidden, line, remote = seq * examples, cfg["hidden"], cfg["line"], cfg["remote"]
    tasks = cfg["task"]
    quad = width // QUADS
    keys = seq + PAD

    load_tok = pltpu.make_async_copy(tok_in, tok, isem.at[0])
    load_cot = pltpu.make_async_copy(cot_in, cot, isem.at[1])
    load_tok.start()
    load_cot.start()

    own = iter(range(64))
    cols = lambda start, size: pl.ds(start, size)
    everything = (slice(None),)
    sources = [(h_tab, [(table, everything)])]
    for j in range(QUADS):
        sources.append(
            (
                h_q[j],
                [
                    (wqkv.at[:, cols(part * width + j * quad, quad)], (slice(None), cols(part * quad, quad)))
                    for part in range(3)
                ],
            )
        )
    sources.append((h_out, [(wout, everything)]))
    groups = tasks if remote else 1
    piece = hidden // (groups * CHUNKS)
    for i in range(CHUNKS):
        sources.append(
            (
                h_fc[i],
                [
                    (
                        wfc.at[:, cols(g * (hidden // groups) + i * piece, piece)],
                        (slice(None), cols(g * piece, piece)),
                    )
                    for g in range(groups)
                ],
            )
        )
    units = []
    base = 0
    if remote:
        t, b = lax.axis_index("task"), lax.axis_index("batch")
        place = {"t": t, "z": b // 2, "c": lax.rem(b, 2), "line": line}
    for at, (held, owns) in enumerate(sources):
        if remote:
            numbered = [(s, w, next(own)) for s, w in owns]
            units.append(Gather(place, held, ssem, rsem, osem, base, numbered))
            base += Gather.semaphores(line)
        else:
            lead = (0, 0, 0) if at > 0 else ()
            units.append(Local(held, osem, [(s, lead + w if at > 0 else w, next(own)) for s, w in owns]))
    fc_units = units[2 + QUADS :]
    units = units[: 2 + QUADS]
    for i in range(CHUNKS):
        units.append(fc_units[i])
        if remote:
            numbered = [(wproj, everything, next(own))] if i == 0 else None
            if i == 0:
                proj_own = numbered
            units.append(GatherRows(place, h_proj, ssem, rsem, osem, base, proj_own, i))
        else:
            step = hidden // CHUNKS
            units.append(
                Local(h_proj, osem, [(wproj.at[pl.ds(i * step, step)], (0, i, 0), next(own))])
            )
    pump = Pump(units)
    pump.begin()
    if remote:
        barrier = pltpu.get_barrier_semaphore()
        mates = [(t, lax.rem(place["z"] + k, line) * 2 + place["c"]) for k in range(1, line)]
        mates += [(t ^ 1, b), (t ^ 2, b), (t, place["z"] * 2 + 1 - place["c"])]
        for mate in mates:
            pl.semaphore_signal(barrier, inc=1, device_id=mate, device_id_type=pl.DeviceIdType.MESH)
        pl.semaphore_wait(barrier, len(mates))
    pump.run(6)

    def each(count, body):
        lax.fori_loop(0, count, lambda i, carry: (body(i), carry)[1], 0)

    def band(i, size):
        return pl.ds(pl.multiple_of(i * size, size), size)

    load_tok.wait()
    load_cot.wait()

    def first_norm(e):
        at = band(e, seq)
        hat, _ = norm_parts(tok[at, :].astype(f32))
        normed[at, :] = (hat * gain1[...] + shift1[...]).astype(bf16)

    each(examples, first_norm)

    pump.ready(0)
    lead = h_tab.shape[:3]
    piece_cols = h_tab.shape[-1]

    for e in range(examples):
        number = ids[e]
        owner, local = number // cfg["group"], lax.rem(number, cfg["group"])
        for z in range(lead[1]):
            for c in range(lead[2]):
                where = (z * lead[2] + c) * piece_cols
                pkv[e, :, where : where + piece_cols] = h_tab[owner, z, c, local]

    def head_keys(e, j, part):
        at = band(e, seq)
        return jnp.concatenate(
            [
                qkv[j, at, part * quad : (part + 1) * quad],
                pkv[e, :, (part - 1) * width + j * quad : (part - 1) * width + (j + 1) * quad],
            ],
            axis=0,
        )

    def from_keys(block, weights):
        flipped = block[:seq].T
        heads = [
            dot_nn(
                flipped[h * HEAD_DIM : (h + 1) * HEAD_DIM], weights[h * keys : h * keys + seq]
            )
            for h in range(QUAD_HEADS)
        ]
        extra = spread_heads(block[seq:]).T
        low = jnp.concatenate(
            [weights[h * keys + seq : (h + 1) * keys] for h in range(QUAD_HEADS)], axis=0
        )
        return jnp.concatenate(heads, axis=0) + dot_nn(extra, low)

    def attend(j, e):
        at = band(e, seq)
        counted = counted_keys(seq, prefix)
        scores = dot_nt(spread_heads(head_keys(e, j, 1)), qkv[j, at, :quad])
        weights, inverse = [], []
        for h in range(QUAD_HEADS):
            score = jnp.where(counted, scores[h * keys : (h + 1) * keys], MASKED)
            top = jnp.max(score, axis=0, keepdims=True)
            exps = jnp.exp(score - top)
            total = jnp.sum(exps, axis=0, keepdims=True)
            lse[j, e, h : h + 1, :] = top + jnp.log(total)
            weights.append(exps.astype(bf16))
            inverse.append(jnp.broadcast_to(1.0 / total, (HEAD_DIM, seq)))
        out = from_keys(head_keys(e, j, 2), jnp.concatenate(weights, axis=0))
        out = out * jnp.concatenate(inverse, axis=0)
        att[at, j * quad : (j + 1) * quad] = out.astype(bf16).T

    half = rows // 2
    for j in range(QUADS):
        pump.ready(1 + j)

        def project(i, j=j):
            at = band(i, half)
            mixed = dot_nn(normed[at, :], rows_of(h_q[j][...]))
            qkv[j, at, :quad] = (mixed[:, :quad] * HEAD_DIM**-0.5).astype(bf16)
            qkv[j, at, quad:] = mixed[:, quad:].astype(bf16)

        each(2, project)
        pump.run(2)
        each(examples, functools.partial(attend, j))
        pump.run(2)

    pump.ready(1 + QUADS)

    def project_out(i):
        at = band(i, half)
        res[at, :] = tok[at, :].astype(f32) + dot_nn(att[at, :], rows_of(h_out[...]))

    each(2, project_out)
    pump.run(2)

    def second_norm(e):
        at = band(e, seq)
        hat, _ = norm_parts(res[at, :])
        normed[at, :] = (hat * gain2[...] + shift2[...]).astype(bf16)

    each(examples, second_norm)

    slope = 0.7978845608028654
    cubic = 0.044715 * slope

    for i in range(CHUNKS):
        pump.ready(2 + QUADS + 2 * i)
        pump.ready(3 + QUADS + 2 * i)

        def feed(r, i=i):
            at = band(r, half)
            w_up = rows_of(h_fc[i][...])
            w_down = rows_of(h_proj[:, i])
            up = dot_nn(normed[at, :], w_up)
            g_act = dot_nt(cot[at, :], w_down)
            square = up * up
            bend = jnp.tanh(up * (slope + cubic * square))
            raised = 0.5 + 0.5 * bend
            active = (up * raised).astype(bf16)
            turn = 0.5 * (1.0 - bend * bend) * (slope + 3.0 * cubic * square)
            g_up = (g_act * (raised + up * turn)).astype(bf16)
            down = dot_nn(active, w_down)
            back = dot_nt(g_up, w_up)
            if i == 0:
                acc[at, :] = down
                gacc[at, :] = back
            else:
                acc[at, :] += down
                gacc[at, :] += back

        each(2, feed)
        pump.run(4)
    pump.finish()

    def second_norm_back(e):
        at = band(e, seq)
        value = res[at, :]
        grad = cot[at, :].astype(f32) + norm_back(value, gain2[...], gacc[at, :])
        cot[at, :] = (value + acc[at, :]).astype(bf16)
        res[at, :] = grad
        normed[at, :] = grad.astype(bf16)

    each(examples, second_norm_back)
    store_block = pltpu.make_async_copy(cot, block_to, isem.at[0])
    store_block.start()

    def project_out_back(i):
        at = band(i, half)
        att[at, :] = dot_nt(normed[at, :], rows_of(h_out[...])).astype(bf16)

    each(2, project_out_back)

    def attend_back(j, e):
        at = band(e, seq)
        counted = counted_keys(seq, prefix)
        queries = qkv[j, at, :quad]
        all_keys = head_keys(e, j, 1)
        g_out = att[at, j * quad : (j + 1) * quad]
        scores = dot_nt(spread_heads(all_keys), queries)
        g_probs = dot_nt(spread_heads(head_keys(e, j, 2)), g_out)
        low, g_low = [], []
        for h in range(QUAD_HEADS):
            score = scores[h * keys : (h + 1) * keys]
            probs = jnp.exp(jnp.where(counted, score - lse[j, e, h : h + 1, :], MASKED))
            g_prob = g_probs[h * keys : (h + 1) * keys]
            inner = jnp.sum(probs * g_prob, axis=0, keepdims=True)
            low.append(probs.astype(bf16))
            g_low.append((probs * (g_prob - inner)).astype(bf16))
        low = jnp.concatenate(low, axis=0)
        g_low = jnp.concatenate(g_low, axis=0)
        g_queries = from_keys(all_keys, g_low).astype(bf16).T
        g_keys = join_heads(dot_nn(g_low, queries), keys)
        g_values = join_heads(dot_nn(low, g_out), keys)
        qkv[j, at, :quad] = g_queries * HEAD_DIM**-0.5
        qkv[j, at, quad : 2 * quad] = g_keys[:seq].astype(bf16)
        qkv[j, at, 2 * quad :] = g_values[:seq].astype(bf16)
        prefix_grad[e, :, j * quad : (j + 1) * quad] = g_keys[seq:]
        prefix_grad[e, :, width + j * quad : width + (j + 1) * quad] = g_values[seq:]

    for j in range(QUADS):
        each(examples, functools.partial(attend_back, j))

        def project_back(i, j=j):
            at = band(i, half)
            back = dot_nt(qkv[j, at, :], rows_of(h_q[j][...]))
            if j == 0:
                acc[at, :] = back
            else:
                acc[at, :] += back

        each(2, project_back)

    def first_norm_back(e):
        at = band(e, seq)
        grad = res[at, :] + norm_back(tok[at, :].astype(f32), gain1[...], acc[at, :])
        tok[at, :] = grad.astype(bf16)

    each(examples, first_norm_back)
    store_grad = pltpu.make_async_copy(tok, grad_to, isem.at[1])
    store_grad.start()
    store_block.wait()
    store_grad.wait()


def run_block(cfg, tokens, cotangent, task_ids, norms, weights, table):
    rows, width, hidden = cfg["seq"] * cfg["examples"], cfg["width"], cfg["hidden"]
    remote, line, tasks = cfg["remote"], cfg["line"], cfg["task"]
    lead = (tasks, line, 2) if remote else (1, 1, 1)
    shard = lambda w, columns: pltpu.VMEM(lead + (w.shape[0], columns), bf16)
    quad = width // QUADS
    if remote:
        held = [pltpu.VMEM(lead + table.shape, bf16)]
        proj = pltpu.VMEM(lead + weights[3].shape, bf16)
    else:
        held = [pltpu.VMEM(table.shape, bf16)]
        proj = pltpu.VMEM((1, CHUNKS, 1, hidden // CHUNKS, width), bf16)
    held += [shard(weights[0], 3 * quad)] * QUADS + [shard(weights[1], width)]
    held += [shard(weights[2], hidden // CHUNKS)] * CHUNKS + [proj]
    count = (2 + QUADS + CHUNKS) * Gather.semaphores(line) + GatherRows.semaphores(line)
    count = count if remote else 1
    whole = pl.BlockSpec(memory_space=pltpu.VMEM)
    hbm = pl.BlockSpec(memory_space=pl.ANY)
    return pl.pallas_call(
        functools.partial(block_kernel, cfg),
        out_shape=(
            jax.ShapeDtypeStruct((rows, width), bf16),
            jax.ShapeDtypeStruct((rows, width), bf16),
            jax.ShapeDtypeStruct((cfg["examples"], PAD, 2 * width), f32),
        ),
        in_specs=[hbm, hbm, pl.BlockSpec(memory_space=pltpu.SMEM)] + [whole] * 4 + [hbm] * 5,
        out_specs=(hbm, hbm, whole),
        scratch_shapes=held
        + [
            pltpu.VMEM((rows, width), bf16),
            pltpu.VMEM((rows, width), bf16),
            pltpu.VMEM((QUADS, rows, 3 * quad), bf16),
            pltpu.VMEM((rows, width), bf16),
            pltpu.VMEM((rows, width), bf16),
            pltpu.VMEM((rows, width), f32),
            pltpu.VMEM((rows, width), f32),
            pltpu.VMEM((rows, width), f32),
            pltpu.VMEM((cfg["examples"], PAD, 2 * width), bf16),
            pltpu.VMEM((QUADS, cfg["examples"], QUAD_HEADS, cfg["seq"]), f32),
            pltpu.SemaphoreType.DMA((count,)),
            pltpu.SemaphoreType.DMA((count,)),
            pltpu.SemaphoreType.DMA((64,)),
            pltpu.SemaphoreType.DMA((2,)),
        ],
        compiler_params=pltpu.CompilerParams(
            collective_id=0 if remote else None,
            has_side_effects=True,
            vmem_limit_bytes=63 * MIB,
        ),
        name="block",
    )(
        tokens.reshape(rows, width),
        cotangent.reshape(rows, width),
        task_ids,
        *[norm.reshape(1, width) for norm in norms],
        *weights,
        table,
    )


def shards(
    tokens,
    cotangent,
    task_ids,
    qkv_weight,
    out_weight,
    fc_weight,
    proj_weight,
    norm1_gain,
    norm1_shift,
    norm2_gain,
    norm2_shift,
    prefix_embed,
    reparam_in,
    reparam_in_bias,
    reparam_out,
    reparam_out_bias,
):
    group_count, batch = lax.axis_size("task"), lax.axis_size("batch")
    task_group, prefix_len, model_width = prefix_embed.shape
    ex_count, seq_len, _ = tokens.shape
    inner = reparam_in.shape[2]
    slot_count = group_count * CAP
    at_batch = lax.axis_index("batch")
    columns = 2 * model_width // batch
    remote = qkv_weight.shape[0] % 16 == 0 and columns % 128 == 0

    pre_act = (
        jnp.einsum("tpd,tdr->tpr", prefix_embed, reparam_in, preferred_element_type=f32)
        + reparam_in_bias.astype(f32)[:, None, :]
    )
    hidden_act = jnp.tanh(pre_act)
    hidden_low = hidden_act.astype(bf16)
    out_part = lax.dynamic_slice_in_dim(reparam_out, at_batch * columns, columns, 2)
    bias_part = lax.dynamic_slice_in_dim(reparam_out_bias, at_batch * columns, columns, 1)
    table = (
        jnp.einsum("tpr,trc->tpc", hidden_low, out_part, preferred_element_type=f32)
        + bias_part.astype(f32)[:, None, :]
    ).astype(bf16)
    table = jnp.pad(table, ((0, 0), (0, PAD - prefix_len), (0, 0)))
    weights = (qkv_weight, out_weight, fc_weight, proj_weight)
    if not remote:
        weights = tuple(lax.all_gather(w, ("task", "batch"), axis=0, tiled=True) for w in weights)
        table = lax.all_gather(
            lax.all_gather(table, "batch", axis=2, tiled=True), "task", axis=0
        )[:, None, None]
    cfg = {
        "seq": seq_len,
        "width": model_width,
        "examples": ex_count,
        "prefix": prefix_len,
        "hidden": fc_weight.shape[1],
        "task": group_count,
        "line": batch // 2,
        "group": task_group,
        "remote": remote,
    }
    block_out, input_grad, grad_prefix = run_block(
        cfg,
        tokens,
        cotangent,
        task_ids,
        (norm1_gain, norm1_shift, norm2_gain, norm2_shift),
        weights,
        table,
    )
    grad_prefix = grad_prefix[:, :prefix_len].reshape(ex_count, -1)

    owners = task_ids // task_group
    local_task = task_ids % task_group
    before = jnp.arange(ex_count)[None, :] < jnp.arange(ex_count)[:, None]
    earlier = jnp.sum((before & (owners[None, :] == owners[:, None])).astype(jnp.int32), axis=1)
    slot_of = owners * CAP + earlier
    slot_hot = slot_of[:, None] == jnp.arange(slot_count)[None, :]
    request = jnp.sum(jnp.where(slot_hot, local_task[:, None] + 1, 0), axis=0) - 1
    received = lax.all_to_all(
        request.reshape(group_count, CAP), "task", split_axis=0, concat_axis=0, tiled=True
    )
    grad_slots = jnp.sum(
        jnp.where(slot_hot[:, :, None], grad_prefix[:, None, :], 0.0), axis=0
    ).astype(bf16)
    incoming = lax.all_to_all(
        grad_slots.reshape(group_count, CAP, -1), "task", split_axis=0, concat_axis=0, tiled=True
    ).astype(f32)
    pick_hot = received.reshape(slot_count)[:, None] == jnp.arange(task_group)[None, :]
    grad_table = jnp.sum(
        jnp.where(pick_hot[:, :, None], incoming.reshape(slot_count, 1, -1), 0.0), axis=0
    )
    grad_table = lax.psum(grad_table, "batch").reshape(task_group, prefix_len, 2 * model_width)

    mine = lambda value, axis: lax.dynamic_slice_in_dim(
        value, at_batch * (value.shape[axis] // batch), value.shape[axis] // batch, axis
    )
    grad_hidden = jnp.einsum(
        "tpc,trc->tpr", grad_table, reparam_out.astype(f32), precision=highest
    )
    grad_pre = grad_hidden * (1.0 - hidden_act * hidden_act)
    grad_out_weight = jnp.einsum(
        "tpr,tpc->trc", mine(hidden_low, 2).astype(f32), grad_table, precision=highest
    )
    grad_out_bias = jnp.sum(mine(grad_table, 2), axis=1)
    grad_in_weight = jnp.einsum(
        "tpd,tpr->tdr", mine(prefix_embed, 2).astype(f32), grad_pre, precision=highest
    )
    grad_in_bias = jnp.sum(mine(grad_pre, 2), axis=1)
    grad_embed = jnp.einsum(
        "tpr,tdr->tpd", grad_pre, mine(reparam_in, 1).astype(f32), precision=highest
    )
    return (
        block_out.reshape(tokens.shape),
        input_grad.reshape(tokens.shape),
        grad_embed,
        grad_in_weight,
        grad_in_bias,
        grad_out_weight,
        grad_out_bias,
    )


def solution(mesh):
    everyone = ("task", "batch")
    return jax.shard_map(
        shards,
        mesh=mesh,
        in_specs=(
            P(everyone, None, None),
            P(everyone, None, None),
            P(everyone),
            P(everyone, None),
            P(everyone, None),
            P(everyone, None),
            P(everyone, None),
            P(),
            P(),
            P(),
            P(),
            P("task", None, None),
            P("task", None, None),
            P("task", None),
            P("task", None, None),
            P("task", None),
        ),
        out_specs=(
            P(everyone, None, None),
            P(everyone, None, None),
            P("task", None, "batch"),
            P("task", "batch", None),
            P("task", "batch"),
            P("task", "batch", None),
            P("task", "batch"),
        ),
        check_vma=False,
    )
```

```python
import functools

import jax
import jax.numpy as jnp
from jax import lax
from jax.experimental import pallas as pl
from jax.experimental.pallas import tpu as pltpu
from jax.sharding import PartitionSpec as P

HEADS = 16
HEAD_DIM = 64
CAP = 2
QUADS = 4
QUAD_HEADS = HEADS // QUADS
PAD = 16
CHUNKS = 4
MASKED = -1e30
MIB = 1024 * 1024

UNITS = ["tab", "q0", "q1", "q2", "q3", "out"] + [f"fc{i}" for i in range(2 * CHUNKS)]
UNITS += [f"p{i}" for i in range(CHUNKS)]
PLACES = {"tab": 1.2, "q0": 0, "q1": 1, "q2": 2, "q3": 3, "out": 4, "p0": 5, "p1": 6, "p2": 7, "p3": 8}
PLACES.update({f"fc{i}": 9 + i for i in range(2 * CHUNKS)})
BY_PLANE = ("q0", "out", "p0")
LINE_LAGS = (0, 1, 2, 3, 3.05)
PLANE_LAGS = (0, 1, 2, 3, 4, 5, 6)

highest = lax.Precision.HIGHEST
epsilon = 1e-05
bf16 = jnp.bfloat16
f32 = jnp.float32
NT_DIMS = (((1,), (1,)), ((), ()))


def dot_nn(left, right):
    return jnp.dot(left, right, preferred_element_type=f32)


def dot_nt(left, right):
    return lax.dot_general(left, right, NT_DIMS, preferred_element_type=f32)


def rows_of(value):
    return value.reshape(-1, value.shape[-1])


class Gather:
    def __init__(self, place, held, ssem, rsem, osem, base, owns, window=(0, None)):
        self.place, self.held = place, held
        self.low, self.high = window[0], window[1] or held.shape[3]
        self.ssem, self.rsem, self.osem, self.base = ssem, rsem, osem, base
        self.owns = owns
        self.line = place["line"]
        self.cut = self.line // 2

    @staticmethod
    def semaphores(line):
        return (line - 1) + 8

    def remote(self, ref, at, target):
        return pltpu.make_async_remote_copy(
            src_ref=ref,
            dst_ref=ref,
            send_sem=self.ssem.at[self.base + at],
            recv_sem=self.rsem.at[self.base + at],
            device_id=target,
            device_id_type=pl.DeviceIdType.MESH,
        )

    def own_copies(self):
        slot = self.held.at[self.place["t"], self.place["z"], self.place["c"]]
        return [
            pltpu.make_async_copy(source, slot.at[where], self.osem.at[index])
            for source, where, index in self.owns
        ]

    def to_line(self, k):
        p = self.place
        target = (p["t"], lax.rem(p["z"] + k, self.line) * 2 + p["c"])
        return self.remote(self.held.at[p["t"], p["z"], p["c"], self.low : self.high], k - 1, target)

    def part(self, flip, first, last, at, target):
        p = self.place
        return self.remote(
            self.held.at[p["t"] ^ flip, first:last, p["c"], self.low : self.high],
            self.line - 1 + at,
            target,
        )

    LAGS = LINE_LAGS
    NAMES = ("x", "y", "xr", "yr", "s0", "s1", "s2", "s3")

    def copy(self, name):
        p, n = self.place, self.line
        at = self.NAMES.index(name)
        if name[0] == "s":
            return self.part(int(name[1]), 0, n, at, (p["t"], p["z"] * 2 + 1 - p["c"]))
        step = 1 if name[0] == "x" else 2
        target = (p["t"] ^ step, p["z"] * 2 + p["c"])
        if name[1:] == "r":
            first, last = (0, self.cut) if step == 1 else (self.cut, n)
            return self.part(3 - step, first, last, at, target)
        return self.part(0, 0, n, at, target)

    def begin(self):
        for copy in self.own_copies():
            copy.start()

    def stage(self, step):
        c = self.copy
        if step == 0:
            for copy in self.own_copies():
                copy.wait()
            for k in range(1, self.line):
                self.to_line(k).start()
        elif step == 1:
            for k in range(1, self.line):
                self.to_line(k).wait_recv()
            c("x").start()
            c("y").start()
            c("s0").start()
        elif step == 2:
            c("x").wait_recv()
            c("yr").start()
            c("s1").start()
            c("y").wait_recv()
            c("xr").start()
            c("s2").start()
        elif step == 3:
            c("xr").wait_recv()
            c("yr").wait_recv()
            c("s3").start()
        elif step == 4:
            for name in ("s0", "s1", "s2", "s3"):
                c(name).wait_recv()

    def finish(self):
        for k in range(1, self.line):
            self.to_line(k).wait_send()
        for name in self.NAMES:
            self.copy(name).wait_send()


class GatherPlane(Gather):
    LAGS = PLANE_LAGS

    @staticmethod
    def semaphores(line):
        return 4 + 2 * (line - 1) + line

    def mate(self, z, c=None):
        p = self.place
        return (p["t"], lax.rem(z + self.line, self.line) * 2 + (p["c"] if c is None else c))

    def plane(self, z, at, target):
        return self.remote(
            self.held.at[
                :, lax.rem(z + self.line, self.line), self.place["c"], self.low : self.high
            ],
            at,
            target,
        )

    def part(self, flip, low, high, at, target):
        p = self.place
        return self.remote(self.held.at[p["t"] ^ flip, p["z"], p["c"], low:high], at, target)

    def copy(self, name):
        p = self.place
        half = (self.low + self.high) // 2
        step = 1 if name[0] == "x" else 2
        target = (p["t"] ^ step, p["z"] * 2 + p["c"])
        if name[1:] == "r":
            low, high = (self.low, half) if step == 1 else (half, self.high)
            return self.part(3 - step, low, high, 1 + step, target)
        return self.part(0, self.low, self.high, step - 1, target)

    def up(self, k):
        return self.plane(self.place["z"] - (k - 1), 3 + k, self.mate(self.place["z"] + 1))

    def down(self, k):
        return self.plane(
            self.place["z"] + (k - 1), 2 + self.line + k, self.mate(self.place["z"] - 1)
        )

    def from_below(self, k):
        return self.plane(self.place["z"] - k, 3 + k, self.mate(self.place["z"] + 1))

    def from_above(self, k):
        return self.plane(
            self.place["z"] + k, 2 + self.line + k, self.mate(self.place["z"] - 1)
        )

    def across(self, z):
        mate = self.mate(self.place["z"], 1 - self.place["c"])
        return self.plane(z, 4 + 2 * (self.line - 1) + z, mate)

    def stage(self, step):
        c, z, last = self.copy, self.place["z"], self.line - 1
        if step == 0:
            for copy in self.own_copies():
                copy.wait()
            c("x").start()
            c("y").start()
        elif step == 1:
            c("x").wait_recv()
            c("yr").start()
            c("y").wait_recv()
            c("xr").start()
        elif step == 2:
            c("xr").wait_recv()
            c("yr").wait_recv()
            pl.when(z < last)(lambda: self.up(1).start())
            pl.when(z > 0)(lambda: self.down(1).start())
            self.across(z).start()
        elif step < 3 + last:
            k = step - 2

            @pl.when(z >= k)
            def _():
                self.from_below(k).wait_recv()
                if k < last:
                    pl.when(z < last)(lambda: self.up(k + 1).start())
                self.across(z - k).start()

            @pl.when(z + k <= last)
            def _():
                self.from_above(k).wait_recv()
                if k < last:
                    pl.when(z > 0)(lambda: self.down(k + 1).start())
                self.across(z + k).start()

        elif step == 3 + last:
            for other in range(self.line):
                self.across(other).wait_recv()

    def finish(self):
        z, last = self.place["z"], self.line - 1
        for name in ("x", "y", "xr", "yr"):
            self.copy(name).wait_send()
        for k in range(1, self.line):
            pl.when((z < last) & (z >= k - 1))(lambda k=k: self.up(k).wait_send())
            pl.when((z > 0) & (z + k - 1 <= last))(lambda k=k: self.down(k).wait_send())
        for other in range(self.line):
            self.across(other).wait_send()


class Local:
    LAGS = LINE_LAGS

    def __init__(self, held, osem, owns):
        self.held, self.osem, self.owns = held, osem, owns

    def own_copies(self):
        return [
            pltpu.make_async_copy(source, self.held.at[where], self.osem.at[index])
            for source, where, index in self.owns
        ]

    def begin(self):
        for copy in self.own_copies():
            copy.start()

    def stage(self, step):
        if step == 4:
            for copy in self.own_copies():
                copy.wait()

    def finish(self):
        pass


class Pump:
    def __init__(self, units, places):
        self.units = units
        keyed = [
            (places[u] + lag, step, u)
            for u in range(len(units))
            for step, lag in enumerate(units[u].LAGS)
        ]
        self.order = [(u, step) for _, step, u in sorted(keyed)]
        self.done = 0

    def begin(self):
        for unit in self.units:
            unit.begin()

    def run(self, count):
        for _ in range(count):
            if self.done < len(self.order):
                u, step = self.order[self.done]
                self.units[u].stage(step)
                self.done += 1

    def ready(self, unit):
        last = self.order.index((unit, len(self.units[unit].LAGS) - 1)) + 1
        self.run(max(0, last - self.done))

    def finish(self):
        self.run(len(self.order))
        for unit in self.units:
            unit.finish()


def norm_parts(value):
    average = jnp.mean(value, -1, keepdims=True)
    centred = value - average
    spread = jnp.mean(centred * centred, -1, keepdims=True)
    inverse = lax.rsqrt(spread + epsilon)
    return centred * inverse, inverse


def norm_back(value, gain, grad):
    hat, inverse = norm_parts(value)
    scaled = grad * gain
    first = jnp.mean(scaled, -1, keepdims=True)
    second = jnp.mean(scaled * hat, -1, keepdims=True)
    return inverse * (scaled - first - hat * second)


def spread_heads(block):
    lane = lax.broadcasted_iota(jnp.int32, (1, block.shape[1]), 1) // HEAD_DIM
    return jnp.concatenate(
        [jnp.where(lane == h, block, jnp.zeros_like(block)) for h in range(QUAD_HEADS)], axis=0
    )


def join_heads(block, rows):
    lane = lax.broadcasted_iota(jnp.int32, (1, block.shape[1]), 1) // HEAD_DIM
    total = block[:rows]
    for h in range(1, QUAD_HEADS):
        total = jnp.where(lane == h, block[h * rows : (h + 1) * rows], total)
    return total


def counted_keys(seq, prefix):
    key = lax.broadcasted_iota(jnp.int32, (seq + PAD, seq), 0)
    query = lax.broadcasted_iota(jnp.int32, (seq + PAD, seq), 1)
    return jnp.where(key < seq, key, jnp.where(key < seq + prefix, 0, seq)) <= query


def block_kernel(cfg, *refs):
    it = iter(refs)
    take = lambda n: [next(it) for _ in range(n)]
    tok_in, cot_in, ids, gain1, shift1, gain2, shift2 = take(7)
    wqkv, wout, wfc, wproj = take(4)
    remote = cfg["remote"]
    if remote:
        embed, in_weight, in_bias, out_weight, out_bias = take(5)
        (out_weight_rows,) = take(1)
        block_to, grad_to, table_to, g_pre_to, own_hid_to, embed_to, bias_to, in_bias_to, kept = take(9)
    else:
        (table,) = take(1)
        block_to, grad_to, prefix_grad, kept = take(4)
    h_tab, h_q0, h_q1, h_q2, h_q3, h_out = take(6)
    h_fc = take(2 * CHUNKS)
    (h_proj,) = take(1)
    tok, cot, qkv, normed, att, res, acc, gacc, pkv, lse = take(10)
    ssem, rsem, osem, isem = take(4)
    keep_sem = take(1)[0]
    if remote:
        prefix_grad, chosen, padded, hid, flat_hid, from_tasks, from_core, from_line, from_half = take(9)
        es_sem, er_sem = take(2)
    h_q = (h_q0, h_q1, h_q2, h_q3)

    seq, width, examples, prefix = cfg["seq"], cfg["width"], cfg["examples"], cfg["prefix"]
    rows, hidden, line = seq * examples, cfg["hidden"], cfg["line"]
    tasks, group = cfg["task"], cfg["group"]
    quad = width // QUADS
    keys = seq + PAD

    load_tok = pltpu.make_async_copy(tok_in, tok, isem.at[0])
    load_cot = pltpu.make_async_copy(cot_in, cot, isem.at[1])
    load_tok.start()
    load_cot.start()
    if remote:
        t, b = lax.axis_index("task"), lax.axis_index("batch")
        place = {"t": t, "z": b // 2, "c": lax.rem(b, 2), "line": line}
        inner = in_weight.shape[2]
        own_inner, in_rows = inner // (2 * line), width // (2 * line)
        share = 2 * width // (2 * line)
        loads = [
            copy
            for k in range(group)
            for copy in (
                pltpu.make_async_copy(
                    in_weight.at[k], qkv.at[k, :, pl.ds(0, inner)], isem.at[2 + 2 * k]
                ),
                pltpu.make_async_copy(
                    out_weight.at[k, :, pl.ds(pl.multiple_of(b * share, 128), share)],
                    qkv.at[k, pl.ds(0, inner), pl.ds(inner, share)],
                    isem.at[3 + 2 * k],
                ),
            )
        ]
        for copy in loads:
            copy.start()

    own = iter(range(128))
    cols = lambda start, size: pl.ds(start, size)
    everything = (slice(None),)
    sources = [(h_tab, [] if remote else [(table, everything)])]
    for j in range(QUADS):
        sources.append(
            (
                h_q[j],
                [
                    (wqkv.at[:, cols(part * width + j * quad, quad)], (slice(None), cols(part * quad, quad)))
                    for part in range(3)
                ],
            )
        )
    sources.append((h_out, [(wout, everything)]))
    groups = tasks if remote else 1
    piece = hidden // (2 * CHUNKS)
    some = piece // groups
    fc_at = 2 + QUADS
    for f in range(2 * CHUNKS):
        sources.append(
            (
                h_fc[f],
                [
                    (
                        wfc.at[:, cols((g * 2 * CHUNKS + f) * some, some)],
                        (slice(None), cols(g * some, some)),
                    )
                    for g in range(groups)
                ],
            )
        )
    units = []
    base = 0
    for at, (held, owns) in enumerate(sources):
        if remote:
            kind = GatherPlane if UNITS[at] in BY_PLANE else Gather
            numbered = [(s, w, next(own)) for s, w in owns]
            units.append(kind(place, held, ssem, rsem, osem, base, numbered))
            base += kind.semaphores(line)
        else:
            lead = (0, 0, 0) if at > 0 else ()
            units.append(
                Local(held, osem, [(s, lead + w if at > 0 else w, next(own)) for s, w in owns])
            )
    fc_units = list(range(fc_at, fc_at + len(h_fc)))
    proj_units = []
    for i in range(CHUNKS):
        proj_units.append(len(units))
        if remote:
            size = wproj.shape[0] // CHUNKS
            at = pl.ds(i * size, size)
            numbered = [(wproj.at[at], (at,), next(own))]
            window = (i * size, (i + 1) * size)
            units.append(Gather(place, h_proj, ssem, rsem, osem, base, numbered, window))
            base += Gather.semaphores(line)
        else:
            size = hidden // CHUNKS
            units.append(
                Local(h_proj, osem, [(wproj.at[pl.ds(i * size, size)], (0, i, 0), next(own))])
            )
    places = [PLACES[n] for n in UNITS]
    pump = Pump(units, places)
    pump.begin()
    if remote:
        barrier = pltpu.get_barrier_semaphore()
        mates = [(t, lax.rem(place["z"] + k, line) * 2 + place["c"]) for k in range(1, line)]
        mates += [(t ^ 1, b), (t ^ 2, b), (t, place["z"] * 2 + 1 - place["c"])]
        for mate in mates:
            pl.semaphore_signal(barrier, inc=1, device_id=mate, device_id_type=pl.DeviceIdType.MESH)
        pl.semaphore_wait(barrier, len(mates))
    pump.run(2)

    def each(count, body):
        lax.fori_loop(0, count, lambda i, carry: (body(i), carry)[1], 0)

    def band(i, size):
        return pl.ds(pl.multiple_of(i * size, size), size)

    if remote:
        for copy in loads:
            copy.wait()
        padded[...] = jnp.zeros_like(padded)
        for k in range(group):
            padded[k, :prefix, :] = embed[k]
        hid[...] = jnp.zeros_like(hid)
        for k in range(group):
            act = jnp.tanh(
                dot_nn(padded[k], qkv[k, :, :inner]) + in_bias[k : k + 1, :].astype(f32)
            )
            hid[k * PAD : (k + 1) * PAD, :] = act
            own_bias = out_bias[:, pl.ds(pl.multiple_of(b * share, 128), share)].astype(f32)
            h_tab[t, place["z"], place["c"], k] = (
                dot_nn(act.astype(bf16), qkv[k, :inner, inner : inner + share])
                + own_bias[k : k + 1, :]
            ).astype(bf16)
        flat_hid[...] = hid[...].T
    load_tok.wait()

    def first_norm(e):
        at = band(e, seq)
        hat, _ = norm_parts(tok[at, :].astype(f32))
        normed[at, :] = (hat * gain1[...] + shift1[...]).astype(bf16)

    each(examples, first_norm)

    pump.ready(0)
    lead = h_tab.shape[:3]
    piece_cols = h_tab.shape[-1]

    for e in range(examples):
        number = ids[e]
        owner, local = number // group, lax.rem(number, group)
        for z in range(lead[1]):
            for c in range(lead[2]):
                where = (z * lead[2] + c) * piece_cols
                pkv[e, :, where : where + piece_cols] = h_tab[owner, z, c, local]

    if remote:
        row = lax.broadcasted_iota(jnp.int32, chosen.shape, 0)
        column = lax.broadcasted_iota(jnp.int32, chosen.shape, 1)
        wanted, given = jnp.full(chosen.shape, -1, jnp.int32), jnp.full(chosen.shape, -2, jnp.int32)
        for k in range(tasks):
            first = k * group * PAD
            number = (t ^ k) * group + (row - first) // PAD
            wanted = jnp.where((row >= first) & (row < first + group * PAD), number, wanted)
        for e in range(examples):
            given = jnp.where(column // PAD == e, ids[e], given)
        met = (wanted == given) & (lax.rem(row, PAD) == lax.rem(column, PAD))
        chosen[...] = met.astype(f32).astype(bf16)

    def head_keys(e, j, part):
        at = band(e, seq)
        return jnp.concatenate(
            [
                qkv[j, at, part * quad : (part + 1) * quad],
                pkv[e, :, (part - 1) * width + j * quad : (part - 1) * width + (j + 1) * quad],
            ],
            axis=0,
        )

    def from_keys(block, weights):
        flipped = block[:seq].T
        heads = [
            dot_nn(
                flipped[h * HEAD_DIM : (h + 1) * HEAD_DIM], weights[h * keys : h * keys + seq]
            )
            for h in range(QUAD_HEADS)
        ]
        extra = spread_heads(block[seq:]).T
        low = jnp.concatenate(
            [weights[h * keys + seq : (h + 1) * keys] for h in range(QUAD_HEADS)], axis=0
        )
        return jnp.concatenate(heads, axis=0) + dot_nn(extra, low)

    def attend(j, e):
        at = band(e, seq)
        counted = counted_keys(seq, prefix)
        scores = dot_nt(spread_heads(head_keys(e, j, 1)), qkv[j, at, :quad])
        weights, inverse = [], []
        for h in range(QUAD_HEADS):
            score = jnp.where(counted, scores[h * keys : (h + 1) * keys], MASKED)
            top = jnp.max(score, axis=0, keepdims=True)
            exps = jnp.exp(score - top)
            total = jnp.sum(exps, axis=0, keepdims=True)
            lse[j, e, h : h + 1, :] = top + jnp.log(total)
            weights.append(exps.astype(bf16))
            inverse.append(jnp.broadcast_to(1.0 / total, (HEAD_DIM, seq)))
        out = from_keys(head_keys(e, j, 2), jnp.concatenate(weights, axis=0))
        out = out * jnp.concatenate(inverse, axis=0)
        att[at, j * quad : (j + 1) * quad] = out.astype(bf16).T

    half = rows // 2
    spill = [
        pltpu.make_async_copy(qkv.at[j, :, pl.ds(0, 2 * quad)], kept.at[j], keep_sem.at[j])
        for j in range(QUADS)
    ]
    fetch = [
        pltpu.make_async_copy(kept.at[j], qkv.at[j, :, pl.ds(0, 2 * quad)], keep_sem.at[j])
        for j in range(QUADS)
    ]
    fetch_tok = pltpu.make_async_copy(tok_in, tok, keep_sem.at[QUADS])
    for j in range(QUADS):
        pump.ready(1 + j)

        def project(i, j=j):
            at = band(i, half)
            mixed = dot_nn(normed[at, :], rows_of(h_q[j][...]))
            qkv[j, at, :quad] = (mixed[:, :quad] * HEAD_DIM**-0.5).astype(bf16)
            qkv[j, at, quad:] = mixed[:, quad:].astype(bf16)

        each(2, project)
        pump.run(2)
        each(examples, functools.partial(attend, j))
        spill[j].start()
        pump.run(2)

    pump.ready(1 + QUADS)

    def project_out(i):
        at = band(i, half)
        res[at, :] = tok[at, :].astype(f32) + dot_nn(att[at, :], rows_of(h_out[...]))

    each(2, project_out)
    pump.run(2)

    def second_norm(e):
        at = band(e, seq)
        hat, _ = norm_parts(res[at, :])
        normed[at, :] = (hat * gain2[...] + shift2[...]).astype(bf16)

    each(examples, second_norm)

    slope = 0.7978845608028654
    cubic = 0.044715 * slope

    load_cot.wait()
    def down_rows(f, at):
        if remote:
            return rows_of(h_proj[:, f // 2, f % 2, :, at])
        return h_proj[0, f // 2, 0, (f % 2) * piece : (f % 2 + 1) * piece, at]

    def g_act_at(f):
        if f % 2 == 0:
            return qkv.at[f // 2, :, pl.ds(0, piece)]
        return (att if f < CHUNKS else tok).at[:, pl.ds((f // 2 % 2) * piece, piece)]

    for copy in spill:
        copy.wait()
    for f in range(2 * CHUNKS):
        if f == 0 or not remote:
            for unit in proj_units:
                pump.ready(unit)

        def back_down(r, f=f):
            at = band(r, half)
            g_act_at(f)[at, :] = dot_nt(cot[at, :], down_rows(f, slice(None))).astype(bf16)

        each(2, back_down)
        pump.run(1)

    for f in range(2 * CHUNKS):
        pump.ready(fc_units[f])
        pump.run(2)

        def feed(r, f=f):
            at = band(r, half)
            up = dot_nn(normed[at, :], rows_of(h_fc[f][...]))
            g_act = g_act_at(f)[at, :].astype(f32)
            square = up * up
            bend = jnp.tanh(up * (slope + cubic * square))
            raised = 0.5 + 0.5 * bend
            active = (up * raised).astype(bf16)
            turn = 0.5 * (1.0 - bend * bend) * (slope + 3.0 * cubic * square)
            g_up = (g_act * (raised + up * turn)).astype(bf16)
            tops = h_fc[f].shape[0] // 2
            for n in range(2):
                to = slice(n * (width // 2), (n + 1) * (width // 2))
                down = dot_nn(active, down_rows(f, to))
                acc[at, to] = down if f == 0 else acc[at, to] + down
            for n in range(2):
                to = slice(n * (width // 2), (n + 1) * (width // 2))
                back = dot_nt(
                    g_up,
                    rows_of(h_fc[f][n * tops : (n + 1) * tops]) if remote else h_fc[f][0, 0, 0, to],
                )
                gacc[at, to] = back if f == 0 else gacc[at, to] + back

        each(2, feed)
    pump.finish()
    for copy in fetch:
        copy.start()
    fetch_tok.start()

    def second_norm_back(e):
        at = band(e, seq)
        value = res[at, :]
        grad = cot[at, :].astype(f32) + norm_back(value, gain2[...], gacc[at, :])
        cot[at, :] = (value + acc[at, :]).astype(bf16)
        res[at, :] = grad
        normed[at, :] = grad.astype(bf16)

    each(examples, second_norm_back)
    store_block = pltpu.make_async_copy(cot, block_to, isem.at[0])
    store_block.start()
    if remote:
        loads = [
            copy
            for k in range(group)
            for copy in (
                pltpu.make_async_copy(
                    out_weight_rows.at[k, :, :, pl.ds(0, width)], h_proj.at[k, :, 0], isem.at[2 + 3 * k]
                ),
                pltpu.make_async_copy(
                    out_weight_rows.at[k, :, :, pl.ds(width, width)], h_proj.at[k, :, 1], isem.at[3 + 3 * k]
                ),
            )
        ]
        for copy in loads:
            copy.start()

    def project_out_back(i):
        at = band(i, half)
        att[at, :] = dot_nt(normed[at, :], rows_of(h_out[...])).astype(bf16)

    each(2, project_out_back)

    for copy in fetch:
        copy.wait()

    def attend_back(j, e):
        at = band(e, seq)
        counted = counted_keys(seq, prefix)
        queries = qkv[j, at, :quad]
        all_keys = head_keys(e, j, 1)
        g_out = att[at, j * quad : (j + 1) * quad]
        scores = dot_nt(spread_heads(all_keys), queries)
        g_probs = dot_nt(spread_heads(head_keys(e, j, 2)), g_out)
        low, g_low = [], []
        for h in range(QUAD_HEADS):
            score = scores[h * keys : (h + 1) * keys]
            probs = jnp.exp(jnp.where(counted, score - lse[j, e, h : h + 1, :], MASKED))
            g_prob = g_probs[h * keys : (h + 1) * keys]
            inner = jnp.sum(probs * g_prob, axis=0, keepdims=True)
            low.append(probs.astype(bf16))
            g_low.append((probs * (g_prob - inner)).astype(bf16))
        low = jnp.concatenate(low, axis=0)
        g_low = jnp.concatenate(g_low, axis=0)
        g_queries = from_keys(all_keys, g_low).astype(bf16).T
        g_keys = join_heads(dot_nn(g_low, queries), keys)
        g_values = join_heads(dot_nn(low, g_out), keys)
        qkv[j, at, :quad] = g_queries * HEAD_DIM**-0.5
        qkv[j, at, quad : 2 * quad] = g_keys[:seq].astype(bf16)
        qkv[j, at, 2 * quad :] = g_values[:seq].astype(bf16)
        at = band(e, PAD)
        kept = prefix_grad.dtype
        prefix_grad[at, j * quad : (j + 1) * quad] = g_keys[seq:].astype(kept)
        prefix_grad[at, width + j * quad : width + (j + 1) * quad] = g_values[seq:].astype(kept)

    block_rows = group * PAD

    def total_at(j, h):
        return gacc.at[pl.ds((2 * j + h) * block_rows, block_rows), pl.ds(0, quad)]

    def piece_at(p):
        return gacc.at[pl.ds(p * block_rows, block_rows), pl.ds(quad, quad)]

    def hop(source, target, at, device):
        return pltpu.make_async_remote_copy(
            src_ref=source,
            dst_ref=target,
            send_sem=es_sem.at[at],
            recv_sem=er_sem.at[at],
            device_id=device,
            device_id_type=pl.DeviceIdType.MESH,
        )

    hops = (tasks - 1) + 1 + (line - 1) + 1

    def to_task(j, k):
        return hop(h_tab.at[k, j], from_tasks.at[j, k - 1], j * hops + k - 1, (t ^ k, b))

    def to_core(j):
        mate = (t, place["z"] * 2 + 1 - place["c"])
        return hop(normed.at[pl.ds(j * 2 * block_rows, block_rows), pl.ds(0, quad)], from_core.at[j], j * hops + tasks - 1, mate)

    def to_line(j, k):
        mate = (t, lax.rem(place["z"] + k, line) * 2 + place["c"])
        source = normed.at[pl.ds((2 * j + 1) * block_rows, block_rows), pl.ds(0, quad)]
        return hop(source, from_line.at[j, k - 1], j * hops + tasks - 1 + k, mate)

    def to_half(j):
        mate = (t, place["z"] * 2 + 1 - place["c"])
        return hop(total_at(j, 0), from_half.at[j], j * hops + hops - 1, mate)

    def exchange(j, step):
        if step == 0:
            for h in range(2):
                start = h * width + j * quad
                totals = dot_nn(chosen[...], prefix_grad[:, start : start + quad])
                total_at(j, h)[...] = totals[:block_rows]
                for k in range(1, tasks):
                    h_tab[k, j, h] = (
                        totals[k * block_rows : (k + 1) * block_rows]
                        .astype(bf16)
                        .reshape(group, PAD, quad)
                    )
            for k in range(1, tasks):
                to_task(j, k).start()
        elif step == 1:
            for k in range(1, tasks):
                to_task(j, k).wait_recv()
            sums = []
            for h in range(2):
                total = total_at(j, h)[...]
                for k in range(1, tasks):
                    total = total + from_tasks[j, k - 1, h].astype(f32).reshape(block_rows, quad)
                sums.append(total)
            first = place["c"] == 0
            total_at(j, 0)[...] = jnp.where(first, sums[0], sums[1])
            normed[2 * j * block_rows : (2 * j + 1) * block_rows, :quad] = jnp.where(
                first, sums[1], sums[0]
            ).astype(bf16)
            to_core(j).start()
        elif step == 2:
            to_core(j).wait_recv()
            total = total_at(j, 0)[...] + from_core[j].astype(f32)
            total_at(j, 0)[...] = total
            normed[(2 * j + 1) * block_rows : (2 * j + 2) * block_rows, :quad] = total.astype(bf16)
            for k in range(1, line):
                to_line(j, k).start()
        elif step == 3:
            total = total_at(j, 0)[...]
            for k in range(1, line):
                to_line(j, k).wait_recv()
                total = total + from_line[j, k - 1].astype(f32)
            total_at(j, 0)[...] = total
            to_half(j).start()
        elif step == 4:
            to_half(j).wait_recv()
            own, other = total_at(j, 0)[...], from_half[j]
            first = place["c"] == 0
            piece_at(j)[...] = jnp.where(first, own, other)
            piece_at(QUADS + j)[...] = jnp.where(first, other, own)

    def exchange_tick(now):
        if remote:
            for step in range(4, -1, -1):
                if 0 <= now - step < QUADS:
                    exchange(now - step, step)

    for j in range(QUADS):
        each(examples, functools.partial(attend_back, j))
        exchange_tick(j)

    for n in range(2):
        for i in range(2):
            at = pl.ds(i * half, half)
            to = pl.ds(n * (width // 2), width // 2)
            lead = h_q[0].shape[0]
            parts = [
                dot_nt(
                    qkv[j, at, :],
                    rows_of(h_q[j][n * (lead // 2) : (n + 1) * (lead // 2)])
                    if remote
                    else h_q[j][0, 0, 0, n * (width // 2) : (n + 1) * (width // 2)],
                )
                for j in range(QUADS)
            ]
            acc[at, to] = (parts[0] + parts[1]) + (parts[2] + parts[3])
            if n == 1:
                exchange_tick(QUADS + i)

    fetch_tok.wait()

    def first_norm_back(e):
        at = band(e, seq)
        grad = res[at, :] + norm_back(tok[at, :].astype(f32), gain1[...], acc[at, :])
        tok[at, :] = grad.astype(bf16)

    each(examples // 2, first_norm_back)
    exchange_tick(QUADS + 2)
    each(examples // 2, lambda e: first_norm_back(e + examples // 2))
    store_grad = pltpu.make_async_copy(tok, grad_to, isem.at[1])
    store_grad.start()

    if remote:
        exchange_tick(QUADS + 3)
        exchange_tick(QUADS + 4)
        for j in range(QUADS):
            for k in range(1, tasks):
                to_task(j, k).wait_send()
            to_core(j).wait_send()
            for k in range(1, line):
                to_line(j, k).wait_send()
            to_half(j).wait_send()
        for copy in loads:
            copy.wait()
        pieces = [piece_at(p)[...] for p in range(2 * QUADS)]
        zeros = jnp.zeros((128 - block_rows, width), bf16)
        table_of = [
            jnp.concatenate(
                [jnp.concatenate(pieces[h * QUADS : (h + 1) * QUADS], axis=1).astype(bf16), zeros],
                axis=0,
            )
            for h in range(2)
        ]
        lane = lax.broadcasted_iota(jnp.int32, (1, 128), 1) // PAD
        flat = jnp.zeros((inner, 128), f32)
        for m in range(group):
            both = dot_nt(rows_of(h_proj[m, :, 0]), table_of[0]) + dot_nt(
                rows_of(h_proj[m, :, 1]), table_of[1]
            )
            flat = jnp.where(lane == m, both, flat)
        act = hid[...]
        g_pre = flat.T * (1.0 - act * act)
        g_low = g_pre.astype(bf16)
        table_to[0], table_to[1] = table_of
        g_pre_to[...] = g_low
        own_hid_to[...] = flat_hid[pl.ds(pl.multiple_of(b * own_inner, 8), own_inner), :]
        embed_to[...] = jnp.concatenate(
            [padded[k, :, pl.ds(pl.multiple_of(b * in_rows, 128), in_rows)] for k in range(group)]
            + [jnp.zeros((128 - block_rows, in_rows), bf16)],
            axis=0,
        ).T
        for m in range(group):
            own_piece = gacc[pl.ds(pl.multiple_of(b * block_rows + m * PAD, 8), PAD), quad : quad + share]
            bias_to[m : m + 1, :] = jnp.sum(own_piece, axis=0, keepdims=True)
            summed = jnp.sum(g_pre[m * PAD : (m + 1) * PAD], axis=0, keepdims=True)
            back = lax.rem(inner - b * own_inner, inner)
            turned = pltpu.roll(jnp.broadcast_to(summed, (8, inner)), back, 1)
            in_bias_to[m : m + 1, :] = turned[:1, :own_inner]
    store_block.wait()
    store_grad.wait()


def run_block(cfg, tokens, cotangent, task_ids, norms, weights, rest):
    rows, width, hidden = cfg["seq"] * cfg["examples"], cfg["width"], cfg["hidden"]
    remote, line, tasks, group = cfg["remote"], cfg["line"], cfg["task"], cfg["group"]
    lead = (tasks, line, 2) if remote else (1, 1, 1)
    shard = lambda w, columns: pltpu.VMEM(lead + (w.shape[0], columns), bf16)
    quad = width // QUADS
    whole = pl.BlockSpec(memory_space=pltpu.VMEM)
    hbm = pl.BlockSpec(memory_space=pl.ANY)
    wide = jax.ShapeDtypeStruct((rows, width), bf16)
    prefix_grad = (cfg["examples"] * PAD, 2 * width)
    if remote:
        share, inner = 2 * width // (2 * line), rest[1].shape[2]
        held = [pltpu.VMEM(lead + (group, PAD, share), bf16)]
        proj = pltpu.VMEM(lead + weights[3].shape, bf16)
        rest = rest + (
            rest[3].reshape(group, line, inner // line, 2 * width),
        )
        rest_specs = [whole, hbm, whole, hbm, whole, hbm]
        outs = [
            wide,
            wide,
            jax.ShapeDtypeStruct((2, 128, width), bf16),
            jax.ShapeDtypeStruct((128, inner), bf16),
            jax.ShapeDtypeStruct((inner // (2 * line), 128), f32),
            jax.ShapeDtypeStruct((width // (2 * line), 128), bf16),
            jax.ShapeDtypeStruct((group, share), f32),
            jax.ShapeDtypeStruct((group, inner // (2 * line)), f32),
        ]
        out_specs = [hbm, hbm] + [whole] * 6
        hops = QUADS * (tasks + line)
        more = [
            pltpu.VMEM(prefix_grad, bf16),
            pltpu.VMEM((tasks * group * PAD, cfg["examples"] * PAD), bf16),
            pltpu.VMEM((group, PAD, width), bf16),
            pltpu.VMEM((128, inner), f32),
            pltpu.VMEM((inner, 128), f32),
            pltpu.VMEM((QUADS, tasks - 1, 2, group, PAD, quad), bf16),
            pltpu.VMEM((QUADS, group * PAD, quad), bf16),
            pltpu.VMEM((QUADS, line - 1, group * PAD, quad), bf16),
            pltpu.VMEM((QUADS, group * PAD, quad), f32),
            pltpu.SemaphoreType.DMA((hops,)),
            pltpu.SemaphoreType.DMA((hops,)),
        ]
    else:
        held = [pltpu.VMEM(rest[0].shape, bf16)]
        proj = pltpu.VMEM((1, CHUNKS, 1, hidden // CHUNKS, width), bf16)
        rest_specs = [hbm]
        outs = [wide, wide, jax.ShapeDtypeStruct(prefix_grad, f32)]
        out_specs = [hbm, hbm, whole]
        more = []
    outs.append(jax.ShapeDtypeStruct((QUADS, rows, 2 * quad), bf16))
    out_specs.append(hbm)
    held += [shard(weights[0], 3 * quad)] * QUADS + [shard(weights[1], width)]
    held += [shard(weights[2], hidden // (2 * CHUNKS))] * (2 * CHUNKS) + [proj]
    count = len(UNITS) * GatherPlane.semaphores(line)
    count = count if remote else 1
    return pl.pallas_call(
        functools.partial(block_kernel, cfg),
        out_shape=outs,
        in_specs=[hbm, hbm, pl.BlockSpec(memory_space=pltpu.SMEM)]
        + [whole] * 4
        + [hbm] * 4
        + rest_specs,
        out_specs=out_specs,
        scratch_shapes=held
        + [
            pltpu.VMEM((rows, width), bf16),
            pltpu.VMEM((rows, width), bf16),
            pltpu.VMEM((QUADS, rows, 3 * quad), bf16),
            pltpu.VMEM((rows, width), bf16),
            pltpu.VMEM((rows, width), bf16),
            pltpu.VMEM((rows, width), f32),
            pltpu.VMEM((rows, width), f32),
            pltpu.VMEM((rows, width), f32),
            pltpu.VMEM((cfg["examples"], PAD, 2 * width), bf16),
            pltpu.VMEM((QUADS, cfg["examples"], QUAD_HEADS, cfg["seq"]), f32),
            pltpu.SemaphoreType.DMA((count,)),
            pltpu.SemaphoreType.DMA((count,)),
            pltpu.SemaphoreType.DMA((128,)),
            pltpu.SemaphoreType.DMA((2 + 3 * group,)),
            pltpu.SemaphoreType.DMA((QUADS + 1,)),
        ]
        + more,
        compiler_params=pltpu.CompilerParams(
            collective_id=0 if remote else None,
            has_side_effects=True,
            vmem_limit_bytes=63 * MIB,
        ),
        name="block",
    )(
        tokens.reshape(rows, width),
        cotangent.reshape(rows, width),
        task_ids,
        *[norm.reshape(1, width) for norm in norms],
        *weights,
        *rest,
    )


def task_kernel(cfg, *refs):
    block_in, grad_in, table, g_pre, own_hid, embed, bias, in_bias, in_weight = refs[:9]
    block_to, grad_to, embed_to, in_to, in_bias_to, out_to, bias_to = refs[9:16]
    own_weight, block_here, grad_here, sems = refs[16:]
    group, width, prefix = cfg["group"], cfg["width"], cfg["prefix"]
    parts = 4
    size = block_in.shape[0] // parts
    own = lax.axis_index("batch")
    copies = []
    for m in range(group):
        copies.append(
            pltpu.make_async_copy(
                in_weight.at[m, pl.ds(pl.multiple_of(own * embed.shape[0], 16), embed.shape[0])],
                own_weight.at[m],
                sems.at[2 * parts + m],
            )
        )
    for i in range(parts):
        at = pl.ds(i * size, size)
        for n, (source, here) in enumerate(((block_in, block_here), (grad_in, grad_here))):
            copies.append(pltpu.make_async_copy(source.at[at], here.at[at], sems.at[2 * i + n]))
    for copy in copies:
        copy.start()
    stores = []
    for i in range(parts):
        at = pl.ds(i * size, size)
        for n, (here, target) in enumerate(((block_here, block_to), (grad_here, grad_to))):
            copies[group + 2 * i + n].wait()
            stores.append(pltpu.make_async_copy(here.at[at], target.at[at], sems.at[2 * i + n]))
            stores[-1].start()
    lane = lax.broadcasted_iota(jnp.int32, (1, 128), 1) // PAD
    for m in range(group):
        left = jnp.where(lane == m, own_hid[...], 0.0).astype(bf16)
        for h in range(2):
            out_to[m, :, h * width : (h + 1) * width] = dot_nn(left, table[h])
        left = jnp.where(lane == m, embed[...].astype(f32), 0.0).astype(bf16)
        in_to[m] = dot_nn(left, g_pre[...])
    in_bias_to[...] = in_bias[...]
    bias_to[...] = bias[...]
    for m in range(group):
        copies[m].wait()
        embed_to[m] = dot_nt(g_pre[m * PAD : (m + 1) * PAD], own_weight[m])[:prefix]
    for copy in stores:
        copy.wait()


def finish_task(cfg, made, in_weight):
    group, inner, width = cfg["group"], in_weight.shape[2], cfg["width"]
    whole = pl.BlockSpec(memory_space=pltpu.VMEM)
    hbm = pl.BlockSpec(memory_space=pl.ANY)
    share = width // (2 * cfg["line"])
    own_inner = inner // (2 * cfg["line"])
    return pl.pallas_call(
        functools.partial(task_kernel, cfg),
        out_shape=(
            jax.ShapeDtypeStruct(made[0].shape, bf16),
            jax.ShapeDtypeStruct(made[1].shape, bf16),
            jax.ShapeDtypeStruct((group, cfg["prefix"], share), f32),
            jax.ShapeDtypeStruct((group, share, inner), f32),
            jax.ShapeDtypeStruct((group, own_inner), f32),
            jax.ShapeDtypeStruct((group, own_inner, 2 * width), f32),
            jax.ShapeDtypeStruct((group, 2 * share), f32),
        ),
        in_specs=[hbm, hbm] + [whole] * 6 + [hbm],
        out_specs=(hbm, hbm) + (whole,) * 5,
        scratch_shapes=[
            pltpu.VMEM((group, share, inner), bf16),
            pltpu.VMEM(made[0].shape, bf16),
            pltpu.VMEM(made[1].shape, bf16),
            pltpu.SemaphoreType.DMA((8 + group,)),
        ],
        compiler_params=pltpu.CompilerParams(vmem_limit_bytes=60 * MIB),
        name="task",
    )(*made, in_weight)


def shards(
    tokens,
    cotangent,
    task_ids,
    qkv_weight,
    out_weight,
    fc_weight,
    proj_weight,
    norm1_gain,
    norm1_shift,
    norm2_gain,
    norm2_shift,
    prefix_embed,
    reparam_in,
    reparam_in_bias,
    reparam_out,
    reparam_out_bias,
):
    group_count, batch = lax.axis_size("task"), lax.axis_size("batch")
    task_group, prefix_len, model_width = prefix_embed.shape
    ex_count, seq_len, _ = tokens.shape
    inner = reparam_in.shape[2]
    slot_count = group_count * CAP
    at_batch = lax.axis_index("batch")
    columns = 2 * model_width // batch
    ff_width = fc_weight.shape[1]
    remote = (
        all(w.shape[0] % 16 == 0 for w in (qkv_weight, out_weight, fc_weight, proj_weight))
        and columns == model_width // QUADS
        and (group_count, batch // 2, task_group) == (4, CHUNKS, QUADS)
        and (2 * inner, ff_width) == (model_width, CHUNKS * model_width)
    )
    weights = (qkv_weight, out_weight, fc_weight, proj_weight)
    norms = (norm1_gain, norm1_shift, norm2_gain, norm2_shift)
    cfg = {
        "seq": seq_len,
        "width": model_width,
        "examples": ex_count,
        "prefix": prefix_len,
        "hidden": ff_width,
        "task": group_count,
        "line": batch // 2,
        "group": task_group,
        "remote": remote,
    }
    if remote:
        rest = (prefix_embed, reparam_in, reparam_in_bias, reparam_out, reparam_out_bias)
        *made, _ = run_block(cfg, tokens, cotangent, task_ids, norms, weights, rest)
        block_out, input_grad, *grads = finish_task(cfg, made, reparam_in)
        return block_out.reshape(tokens.shape), input_grad.reshape(tokens.shape), *grads

    pre_act = (
        jnp.einsum("tpd,tdr->tpr", prefix_embed, reparam_in, preferred_element_type=f32)
        + reparam_in_bias.astype(f32)[:, None, :]
    )
    hidden_act = jnp.tanh(pre_act)
    hidden_low = hidden_act.astype(bf16)
    out_part = lax.dynamic_slice_in_dim(reparam_out, at_batch * columns, columns, 2)
    bias_part = lax.dynamic_slice_in_dim(reparam_out_bias, at_batch * columns, columns, 1)
    table = (
        jnp.einsum("tpr,trc->tpc", hidden_low, out_part, preferred_element_type=f32)
        + bias_part.astype(f32)[:, None, :]
    ).astype(bf16)
    table = jnp.pad(table, ((0, 0), (0, PAD - prefix_len), (0, 0)))
    weights = tuple(lax.all_gather(w, ("task", "batch"), axis=0, tiled=True) for w in weights)
    table = lax.all_gather(
        lax.all_gather(table, "batch", axis=2, tiled=True), "task", axis=0
    )[:, None, None]
    block_out, input_grad, grad_prefix, _ = run_block(
        cfg, tokens, cotangent, task_ids, norms, weights, (table,)
    )
    grad_prefix = grad_prefix.reshape(ex_count, PAD, -1)[:, :prefix_len].reshape(ex_count, -1)

    owners = task_ids // task_group
    local_task = task_ids % task_group
    before = jnp.arange(ex_count)[None, :] < jnp.arange(ex_count)[:, None]
    earlier = jnp.sum((before & (owners[None, :] == owners[:, None])).astype(jnp.int32), axis=1)
    slot_of = owners * CAP + earlier
    slot_hot = slot_of[:, None] == jnp.arange(slot_count)[None, :]
    request = jnp.sum(jnp.where(slot_hot, local_task[:, None] + 1, 0), axis=0) - 1
    received = lax.all_to_all(
        request.reshape(group_count, CAP), "task", split_axis=0, concat_axis=0, tiled=True
    )
    grad_slots = jnp.sum(
        jnp.where(slot_hot[:, :, None], grad_prefix[:, None, :], 0.0), axis=0
    ).astype(bf16)
    incoming = lax.all_to_all(
        grad_slots.reshape(group_count, CAP, -1), "task", split_axis=0, concat_axis=0, tiled=True
    ).astype(f32)
    pick_hot = received.reshape(slot_count)[:, None] == jnp.arange(task_group)[None, :]
    grad_table = jnp.sum(
        jnp.where(pick_hot[:, :, None], incoming.reshape(slot_count, 1, -1), 0.0), axis=0
    )
    grad_table = lax.psum(grad_table, "batch").reshape(task_group, prefix_len, 2 * model_width)

    mine = lambda value, axis: lax.dynamic_slice_in_dim(
        value, at_batch * (value.shape[axis] // batch), value.shape[axis] // batch, axis
    )
    grad_hidden = jnp.einsum(
        "tpc,trc->tpr", grad_table, reparam_out.astype(f32), precision=highest
    )
    grad_pre = grad_hidden * (1.0 - hidden_act * hidden_act)
    grad_out_weight = jnp.einsum(
        "tpr,tpc->trc", mine(hidden_low, 2).astype(f32), grad_table, precision=highest
    )
    grad_out_bias = jnp.sum(mine(grad_table, 2), axis=1)
    grad_in_weight = jnp.einsum(
        "tpd,tpr->tdr", mine(prefix_embed, 2).astype(f32), grad_pre, precision=highest
    )
    grad_in_bias = jnp.sum(mine(grad_pre, 2), axis=1)
    grad_embed = jnp.einsum(
        "tpr,tdr->tpd", grad_pre, mine(reparam_in, 1).astype(f32), precision=highest
    )
    return (
        block_out.reshape(tokens.shape),
        input_grad.reshape(tokens.shape),
        grad_embed,
        grad_in_weight,
        grad_in_bias,
        grad_out_weight,
        grad_out_bias,
    )


def solution(mesh):
    everyone = ("task", "batch")
    return jax.shard_map(
        shards,
        mesh=mesh,
        in_specs=(
            P(everyone, None, None),
            P(everyone, None, None),
            P(everyone),
            P(everyone, None),
            P(everyone, None),
            P(everyone, None),
            P(everyone, None),
            P(),
            P(),
            P(),
            P(),
            P("task", None, None),
            P("task", None, None),
            P("task", None),
            P("task", None, None),
            P("task", None),
        ),
        out_specs=(
            P(everyone, None, None),
            P(everyone, None, None),
            P("task", None, "batch"),
            P("task", "batch", None),
            P("task", "batch"),
            P("task", "batch", None),
            P("task", "batch"),
        ),
        check_vma=False,
    )
```

```python
import functools

import jax
import jax.numpy as jnp
from jax import lax
from jax.experimental import pallas as pl
from jax.experimental.pallas import tpu as pltpu
from jax.sharding import PartitionSpec as P

HEADS = 16
HEAD_DIM = 64
CAP = 2
QUADS = 4
QUAD_HEADS = HEADS // QUADS
PAD = 16
CHUNKS = 4
MASKED = -1e30
MIB = 1024 * 1024

UNITS = ["tab", "q0", "q1", "q2", "q3", "out"] + [f"fc{i}" for i in range(2 * CHUNKS)]
UNITS += [f"p{i}" for i in range(CHUNKS)]
PLACES = {"tab": 1.2, "q0": 0, "q1": 1, "q2": 2, "q3": 3, "out": 4, "p0": 5, "p1": 6, "p2": 7, "p3": 8}
PLACES.update({f"fc{i}": 9 + i for i in range(2 * CHUNKS)})
BY_PLANE = ("q0", "out", "p0", "p2")
LINE_LAGS = (0, 1, 2, 3, 4)
PLANE_LAGS = (0, 1, 2, 3, 4, 5, 6)

highest = lax.Precision.HIGHEST
epsilon = 1e-05
bf16 = jnp.bfloat16
f32 = jnp.float32
NT_DIMS = (((1,), (1,)), ((), ()))


def dot_nn(left, right):
    return jnp.dot(left, right, preferred_element_type=f32)


def dot_nt(left, right):
    return lax.dot_general(left, right, NT_DIMS, preferred_element_type=f32)


def rows_of(value):
    return value.reshape(-1, value.shape[-1])


class Gather:
    def __init__(self, place, held, ssem, rsem, osem, base, owns, window=(0, None)):
        self.place, self.held = place, held
        self.low, self.high = window[0], window[1] or held.shape[3]
        self.ssem, self.rsem, self.osem, self.base = ssem, rsem, osem, base
        self.owns = owns
        self.line = place["line"]
        self.cut = self.line // 2

    @staticmethod
    def semaphores(line):
        return (line - 1) + 8

    def remote(self, ref, at, target):
        return pltpu.make_async_remote_copy(
            src_ref=ref,
            dst_ref=ref,
            send_sem=self.ssem.at[self.base + at],
            recv_sem=self.rsem.at[self.base + at],
            device_id=target,
            device_id_type=pl.DeviceIdType.MESH,
        )

    def own_copies(self):
        slot = self.held.at[self.place["t"], self.place["z"], self.place["c"]]
        return [
            pltpu.make_async_copy(source, slot.at[where], self.osem.at[index])
            for source, where, index in self.owns
        ]

    def to_line(self, k):
        p = self.place
        target = (p["t"], lax.rem(p["z"] + k, self.line) * 2 + p["c"])
        return self.remote(self.held.at[p["t"], p["z"], p["c"], self.low : self.high], k - 1, target)

    def part(self, flip, first, last, at, target):
        p = self.place
        return self.remote(
            self.held.at[p["t"] ^ flip, first:last, p["c"], self.low : self.high],
            self.line - 1 + at,
            target,
        )

    LAGS = LINE_LAGS
    NAMES = ("x", "y", "xr", "yr", "s0", "s1", "s2", "s3")

    def copy(self, name):
        p, n = self.place, self.line
        at = self.NAMES.index(name)
        if name[0] == "s":
            return self.part(int(name[1]), 0, n, at, (p["t"], p["z"] * 2 + 1 - p["c"]))
        step = 1 if name[0] == "x" else 2
        target = (p["t"] ^ step, p["z"] * 2 + p["c"])
        if name[1:] == "r":
            first, last = (0, self.cut) if step == 1 else (self.cut, n)
            return self.part(3 - step, first, last, at, target)
        return self.part(0, 0, n, at, target)

    def begin(self):
        for copy in self.own_copies():
            copy.start()

    def stage(self, step):
        c = self.copy
        if step == 0:
            for copy in self.own_copies():
                copy.wait()
            for k in range(1, self.line):
                self.to_line(k).start()
        elif step == 1:
            for k in range(1, self.line):
                self.to_line(k).wait_recv()
            c("x").start()
            c("y").start()
            c("s0").start()
        elif step == 2:
            c("x").wait_recv()
            c("yr").start()
            c("s1").start()
            c("y").wait_recv()
            c("xr").start()
            c("s2").start()
        elif step == 3:
            c("xr").wait_recv()
            c("yr").wait_recv()
            c("s3").start()
        elif step == 4:
            for name in ("s0", "s1", "s2", "s3"):
                c(name).wait_recv()

    def finish(self):
        for k in range(1, self.line):
            self.to_line(k).wait_send()
        for name in self.NAMES:
            self.copy(name).wait_send()


class GatherPlane(Gather):
    LAGS = PLANE_LAGS

    @staticmethod
    def semaphores(line):
        return 4 + 2 * (line - 1) + line

    def mate(self, z, c=None):
        p = self.place
        return (p["t"], lax.rem(z + self.line, self.line) * 2 + (p["c"] if c is None else c))

    def plane(self, z, at, target):
        return self.remote(
            self.held.at[
                :, lax.rem(z + self.line, self.line), self.place["c"], self.low : self.high
            ],
            at,
            target,
        )

    def part(self, flip, low, high, at, target):
        p = self.place
        return self.remote(self.held.at[p["t"] ^ flip, p["z"], p["c"], low:high], at, target)

    def copy(self, name):
        p = self.place
        half = (self.low + self.high) // 2
        step = 1 if name[0] == "x" else 2
        target = (p["t"] ^ step, p["z"] * 2 + p["c"])
        if name[1:] == "r":
            low, high = (self.low, half) if step == 1 else (half, self.high)
            return self.part(3 - step, low, high, 1 + step, target)
        return self.part(0, self.low, self.high, step - 1, target)

    def up(self, k):
        return self.plane(self.place["z"] - (k - 1), 3 + k, self.mate(self.place["z"] + 1))

    def down(self, k):
        return self.plane(
            self.place["z"] + (k - 1), 2 + self.line + k, self.mate(self.place["z"] - 1)
        )

    def from_below(self, k):
        return self.plane(self.place["z"] - k, 3 + k, self.mate(self.place["z"] + 1))

    def from_above(self, k):
        return self.plane(
            self.place["z"] + k, 2 + self.line + k, self.mate(self.place["z"] - 1)
        )

    def across(self, z):
        mate = self.mate(self.place["z"], 1 - self.place["c"])
        return self.plane(z, 4 + 2 * (self.line - 1) + z, mate)

    def stage(self, step):
        c, z, last = self.copy, self.place["z"], self.line - 1
        if step == 0:
            for copy in self.own_copies():
                copy.wait()
            c("x").start()
            c("y").start()
        elif step == 1:
            c("x").wait_recv()
            c("yr").start()
            c("y").wait_recv()
            c("xr").start()
        elif step == 2:
            c("xr").wait_recv()
            c("yr").wait_recv()
            pl.when(z < last)(lambda: self.up(1).start())
            pl.when(z > 0)(lambda: self.down(1).start())
            self.across(z).start()
        elif step < 3 + last:
            k = step - 2

            @pl.when(z >= k)
            def _():
                self.from_below(k).wait_recv()
                if k < last:
                    pl.when(z < last)(lambda: self.up(k + 1).start())
                self.across(z - k).start()

            @pl.when(z + k <= last)
            def _():
                self.from_above(k).wait_recv()
                if k < last:
                    pl.when(z > 0)(lambda: self.down(k + 1).start())
                self.across(z + k).start()

        elif step == 3 + last:
            for other in range(self.line):
                self.across(other).wait_recv()

    def finish(self):
        z, last = self.place["z"], self.line - 1
        for name in ("x", "y", "xr", "yr"):
            self.copy(name).wait_send()
        for k in range(1, self.line):
            pl.when((z < last) & (z >= k - 1))(lambda k=k: self.up(k).wait_send())
            pl.when((z > 0) & (z + k - 1 <= last))(lambda k=k: self.down(k).wait_send())
        for other in range(self.line):
            self.across(other).wait_send()


class Local:
    LAGS = LINE_LAGS

    def __init__(self, held, osem, owns):
        self.held, self.osem, self.owns = held, osem, owns

    def own_copies(self):
        return [
            pltpu.make_async_copy(source, self.held.at[where], self.osem.at[index])
            for source, where, index in self.owns
        ]

    def begin(self):
        for copy in self.own_copies():
            copy.start()

    def stage(self, step):
        if step == 4:
            for copy in self.own_copies():
                copy.wait()

    def finish(self):
        pass


class Pump:
    def __init__(self, units, places):
        self.units = units
        keyed = [
            (places[u] + lag, step, u)
            for u in range(len(units))
            for step, lag in enumerate(units[u].LAGS)
        ]
        self.order = [(u, step) for _, step, u in sorted(keyed)]
        self.done = 0

    def begin(self):
        for unit in self.units:
            unit.begin()

    def run(self, count):
        for _ in range(count):
            if self.done < len(self.order):
                u, step = self.order[self.done]
                self.units[u].stage(step)
                self.done += 1

    def ready(self, unit):
        last = self.order.index((unit, len(self.units[unit].LAGS) - 1)) + 1
        self.run(max(0, last - self.done))

    def finish(self):
        self.run(len(self.order))
        for unit in self.units:
            unit.finish()


def norm_parts(value):
    average = jnp.mean(value, -1, keepdims=True)
    centred = value - average
    spread = jnp.mean(centred * centred, -1, keepdims=True)
    inverse = lax.rsqrt(spread + epsilon)
    return centred * inverse, inverse


def norm_back(value, gain, grad):
    hat, inverse = norm_parts(value)
    scaled = grad * gain
    first = jnp.mean(scaled, -1, keepdims=True)
    second = jnp.mean(scaled * hat, -1, keepdims=True)
    return inverse * (scaled - first - hat * second)


def spread_heads(block):
    lane = lax.broadcasted_iota(jnp.int32, (1, block.shape[1]), 1) // HEAD_DIM
    return jnp.concatenate(
        [jnp.where(lane == h, block, jnp.zeros_like(block)) for h in range(QUAD_HEADS)], axis=0
    )


def join_heads(block, rows):
    lane = lax.broadcasted_iota(jnp.int32, (1, block.shape[1]), 1) // HEAD_DIM
    total = block[:rows]
    for h in range(1, QUAD_HEADS):
        total = jnp.where(lane == h, block[h * rows : (h + 1) * rows], total)
    return total


def counted_keys(seq, prefix):
    key = lax.broadcasted_iota(jnp.int32, (seq + PAD, seq), 0)
    query = lax.broadcasted_iota(jnp.int32, (seq + PAD, seq), 1)
    return jnp.where(key < seq, key, jnp.where(key < seq + prefix, 0, seq)) <= query


def block_kernel(cfg, *refs):
    it = iter(refs)
    take = lambda n: [next(it) for _ in range(n)]
    tok_in, cot_in, ids, gain1, shift1, gain2, shift2 = take(7)
    wqkv, wout, wfc, wproj = take(4)
    remote = cfg["remote"]
    if remote:
        embed, in_weight, in_bias, out_weight, out_bias = take(5)
        (out_weight_rows,) = take(1)
        block_to, grad_to, table_to, g_pre_to, own_hid_to, embed_to, bias_to, in_bias_to, kept = take(9)
    else:
        (table,) = take(1)
        block_to, grad_to, prefix_grad, kept = take(4)
    h_tab, h_q0, h_q1, h_q2, h_q3, h_out = take(6)
    h_fc = take(2 * CHUNKS)
    (h_proj,) = take(1)
    tok, cot, qkv, normed, att, res, acc, gacc, pkv, lse = take(10)
    ssem, rsem, osem, isem = take(4)
    keep_sem = take(1)[0]
    if remote:
        prefix_grad, chosen, padded, hid, flat_hid, from_tasks, from_core, from_line, from_half = take(9)
        es_sem, er_sem = take(2)
    h_q = (h_q0, h_q1, h_q2, h_q3)

    seq, width, examples, prefix = cfg["seq"], cfg["width"], cfg["examples"], cfg["prefix"]
    rows, hidden, line = seq * examples, cfg["hidden"], cfg["line"]
    tasks, group = cfg["task"], cfg["group"]
    quad = width // QUADS
    keys = seq + PAD

    load_tok = pltpu.make_async_copy(tok_in, tok, isem.at[0])
    load_cot = pltpu.make_async_copy(cot_in, cot, isem.at[1])
    load_tok.start()
    load_cot.start()
    if remote:
        t, b = lax.axis_index("task"), lax.axis_index("batch")
        place = {"t": t, "z": b // 2, "c": lax.rem(b, 2), "line": line}
        inner = in_weight.shape[2]
        own_inner, in_rows = inner // (2 * line), width // (2 * line)
        share = 2 * width // (2 * line)
        loads = [
            copy
            for k in range(group)
            for copy in (
                pltpu.make_async_copy(
                    in_weight.at[k], qkv.at[k, :, pl.ds(0, inner)], isem.at[2 + 2 * k]
                ),
                pltpu.make_async_copy(
                    out_weight.at[k, :, pl.ds(pl.multiple_of(b * share, 128), share)],
                    qkv.at[k, pl.ds(0, inner), pl.ds(inner, share)],
                    isem.at[3 + 2 * k],
                ),
            )
        ]
        for copy in loads:
            copy.start()

    own = iter(range(128))
    cols = lambda start, size: pl.ds(start, size)
    everything = (slice(None),)
    sources = [(h_tab, [] if remote else [(table, everything)])]
    for j in range(QUADS):
        sources.append(
            (
                h_q[j],
                [
                    (wqkv.at[:, cols(part * width + j * quad, quad)], (slice(None), cols(part * quad, quad)))
                    for part in range(3)
                ],
            )
        )
    sources.append((h_out, [(wout, everything)]))
    groups = tasks if remote else 1
    piece = hidden // (2 * CHUNKS)
    some = piece // groups
    fc_at = 2 + QUADS
    for f in range(2 * CHUNKS):
        sources.append(
            (
                h_fc[f],
                [
                    (
                        wfc.at[:, cols((g * 2 * CHUNKS + f) * some, some)],
                        (slice(None), cols(g * some, some)),
                    )
                    for g in range(groups)
                ],
            )
        )
    units = []
    base = 0
    for at, (held, owns) in enumerate(sources):
        if remote:
            kind = GatherPlane if UNITS[at] in BY_PLANE else Gather
            numbered = [(s, w, next(own)) for s, w in owns]
            units.append(kind(place, held, ssem, rsem, osem, base, numbered))
            base += kind.semaphores(line)
        else:
            lead = (0, 0, 0) if at > 0 else ()
            units.append(
                Local(held, osem, [(s, lead + w if at > 0 else w, next(own)) for s, w in owns])
            )
    fc_units = list(range(fc_at, fc_at + len(h_fc)))
    proj_units = []
    for i in range(CHUNKS):
        proj_units.append(len(units))
        if remote:
            size = wproj.shape[0] // CHUNKS
            at = pl.ds(i * size, size)
            numbered = [(wproj.at[at], (at,), next(own))]
            window = (i * size, (i + 1) * size)
            units.append(Gather(place, h_proj, ssem, rsem, osem, base, numbered, window))
            base += Gather.semaphores(line)
        else:
            size = hidden // CHUNKS
            units.append(
                Local(h_proj, osem, [(wproj.at[pl.ds(i * size, size)], (0, i, 0), next(own))])
            )
    places = [PLACES[n] for n in UNITS]
    pump = Pump(units, places)
    pump.begin()
    if remote:
        barrier = pltpu.get_barrier_semaphore()
        mates = [(t, lax.rem(place["z"] + k, line) * 2 + place["c"]) for k in range(1, line)]
        mates += [(t ^ 1, b), (t ^ 2, b), (t, place["z"] * 2 + 1 - place["c"])]
        for mate in mates:
            pl.semaphore_signal(barrier, inc=1, device_id=mate, device_id_type=pl.DeviceIdType.MESH)
        pl.semaphore_wait(barrier, len(mates))
    pump.run(2)

    def each(count, body):
        lax.fori_loop(0, count, lambda i, carry: (body(i), carry)[1], 0)

    def band(i, size):
        return pl.ds(pl.multiple_of(i * size, size), size)

    if remote:
        for copy in loads:
            copy.wait()
        padded[...] = jnp.zeros_like(padded)
        for k in range(group):
            padded[k, :prefix, :] = embed[k]
        hid[...] = jnp.zeros_like(hid)
        for k in range(group):
            act = jnp.tanh(
                dot_nn(padded[k], qkv[k, :, :inner]) + in_bias[k : k + 1, :].astype(f32)
            )
            hid[k * PAD : (k + 1) * PAD, :] = act
            own_bias = out_bias[:, pl.ds(pl.multiple_of(b * share, 128), share)].astype(f32)
            h_tab[t, place["z"], place["c"], k] = (
                dot_nn(act.astype(bf16), qkv[k, :inner, inner : inner + share])
                + own_bias[k : k + 1, :]
            ).astype(bf16)
        flat_hid[...] = hid[...].T
    load_tok.wait()

    def first_norm(e):
        at = band(e, seq)
        hat, _ = norm_parts(tok[at, :].astype(f32))
        normed[at, :] = (hat * gain1[...] + shift1[...]).astype(bf16)

    each(examples, first_norm)

    pump.ready(0)
    lead = h_tab.shape[:3]
    piece_cols = h_tab.shape[-1]

    for e in range(examples):
        number = ids[e]
        owner, local = number // group, lax.rem(number, group)
        for z in range(lead[1]):
            for c in range(lead[2]):
                where = (z * lead[2] + c) * piece_cols
                pkv[e, :, where : where + piece_cols] = h_tab[owner, z, c, local]

    if remote:
        row = lax.broadcasted_iota(jnp.int32, chosen.shape, 0)
        column = lax.broadcasted_iota(jnp.int32, chosen.shape, 1)
        wanted, given = jnp.full(chosen.shape, -1, jnp.int32), jnp.full(chosen.shape, -2, jnp.int32)
        for k in range(tasks):
            first = k * group * PAD
            number = (t ^ k) * group + (row - first) // PAD
            wanted = jnp.where((row >= first) & (row < first + group * PAD), number, wanted)
        for e in range(examples):
            given = jnp.where(column // PAD == e, ids[e], given)
        met = (wanted == given) & (lax.rem(row, PAD) == lax.rem(column, PAD))
        chosen[...] = met.astype(f32).astype(bf16)

    def head_keys(e, j, part):
        at = band(e, seq)
        return jnp.concatenate(
            [
                qkv[j, at, part * quad : (part + 1) * quad],
                pkv[e, :, (part - 1) * width + j * quad : (part - 1) * width + (j + 1) * quad],
            ],
            axis=0,
        )

    def from_keys(block, weights):
        flipped = block[:seq].T
        heads = [
            dot_nn(
                flipped[h * HEAD_DIM : (h + 1) * HEAD_DIM], weights[h * keys : h * keys + seq]
            )
            for h in range(QUAD_HEADS)
        ]
        extra = spread_heads(block[seq:]).T
        low = jnp.concatenate(
            [weights[h * keys + seq : (h + 1) * keys] for h in range(QUAD_HEADS)], axis=0
        )
        return jnp.concatenate(heads, axis=0) + dot_nn(extra, low)

    def attend(j, e):
        at = band(e, seq)
        counted = counted_keys(seq, prefix)
        scores = dot_nt(spread_heads(head_keys(e, j, 1)), qkv[j, at, :quad])
        weights, inverse = [], []
        for h in range(QUAD_HEADS):
            score = jnp.where(counted, scores[h * keys : (h + 1) * keys], MASKED)
            top = jnp.max(score, axis=0, keepdims=True)
            exps = jnp.exp(score - top)
            total = jnp.sum(exps, axis=0, keepdims=True)
            lse[j, e, h : h + 1, :] = top + jnp.log(total)
            weights.append(exps.astype(bf16))
            inverse.append(jnp.broadcast_to(1.0 / total, (HEAD_DIM, seq)))
        out = from_keys(head_keys(e, j, 2), jnp.concatenate(weights, axis=0))
        out = out * jnp.concatenate(inverse, axis=0)
        att[at, j * quad : (j + 1) * quad] = out.astype(bf16).T

    half = rows // 2
    spill = [
        pltpu.make_async_copy(qkv.at[j, :, pl.ds(0, 2 * quad)], kept.at[j], keep_sem.at[j])
        for j in range(QUADS)
    ]
    fetch = [
        pltpu.make_async_copy(kept.at[j], qkv.at[j, :, pl.ds(0, 2 * quad)], keep_sem.at[j])
        for j in range(QUADS)
    ]
    fetch_tok = pltpu.make_async_copy(tok_in, tok, keep_sem.at[QUADS])
    for j in range(QUADS):
        pump.ready(1 + j)

        def project(i, j=j):
            at = band(i, half)
            mixed = dot_nn(normed[at, :], rows_of(h_q[j][...]))
            qkv[j, at, :quad] = (mixed[:, :quad] * HEAD_DIM**-0.5).astype(bf16)
            qkv[j, at, quad:] = mixed[:, quad:].astype(bf16)

        each(2, project)
        pump.run(2)
        each(examples, functools.partial(attend, j))
        spill[j].start()
        pump.run(2)

    pump.ready(1 + QUADS)

    def project_out(i):
        at = band(i, half)
        res[at, :] = tok[at, :].astype(f32) + dot_nn(att[at, :], rows_of(h_out[...]))

    each(2, project_out)
    pump.run(2)

    def second_norm(e):
        at = band(e, seq)
        hat, _ = norm_parts(res[at, :])
        normed[at, :] = (hat * gain2[...] + shift2[...]).astype(bf16)

    each(examples, second_norm)

    slope = 0.7978845608028654
    cubic = 0.044715 * slope

    load_cot.wait()
    def down_rows(f, at):
        if remote:
            return rows_of(h_proj[:, f // 2, f % 2, :, at])
        return h_proj[0, f // 2, 0, (f % 2) * piece : (f % 2 + 1) * piece, at]

    def g_act_at(f):
        if f % 2 == 0:
            return qkv.at[f // 2, :, pl.ds(0, piece)]
        return (att if f < CHUNKS else tok).at[:, pl.ds((f // 2 % 2) * piece, piece)]

    for copy in spill:
        copy.wait()
    for f in range(2 * CHUNKS):
        if f == 0 or not remote:
            for unit in proj_units:
                pump.ready(unit)

        def back_down(r, f=f):
            at = band(r, half)
            g_act_at(f)[at, :] = dot_nt(cot[at, :], down_rows(f, slice(None))).astype(bf16)

        each(2, back_down)
        pump.run(1)

    for f in range(2 * CHUNKS):
        pump.ready(fc_units[f])
        pump.run(3)

        def feed(r, f=f):
            at = band(r, half)
            up = dot_nn(normed[at, :], rows_of(h_fc[f][...]))
            g_act = g_act_at(f)[at, :].astype(f32)
            square = up * up
            bend = jnp.tanh(up * (slope + cubic * square))
            raised = 0.5 + 0.5 * bend
            active = (up * raised).astype(bf16)
            turn = 0.5 * (1.0 - bend * bend) * (slope + 3.0 * cubic * square)
            g_up = (g_act * (raised + up * turn)).astype(bf16)
            tops = h_fc[f].shape[0] // 2
            for n in range(2):
                to = slice(n * (width // 2), (n + 1) * (width // 2))
                down = dot_nn(active, down_rows(f, to))
                acc[at, to] = down if f == 0 else acc[at, to] + down
            for n in range(2):
                to = slice(n * (width // 2), (n + 1) * (width // 2))
                back = dot_nt(
                    g_up,
                    rows_of(h_fc[f][n * tops : (n + 1) * tops]) if remote else h_fc[f][0, 0, 0, to],
                )
                gacc[at, to] = back if f == 0 else gacc[at, to] + back

        each(2, feed)
    pump.finish()
    for copy in fetch:
        copy.start()
    fetch_tok.start()

    def second_norm_back(e):
        at = band(e, seq)
        value = res[at, :]
        grad = cot[at, :].astype(f32) + norm_back(value, gain2[...], gacc[at, :])
        cot[at, :] = (value + acc[at, :]).astype(bf16)
        res[at, :] = grad
        normed[at, :] = grad.astype(bf16)

    each(examples, second_norm_back)
    store_block = pltpu.make_async_copy(cot, block_to, isem.at[0])
    store_block.start()
    if remote:
        loads = [
            copy
            for k in range(group)
            for copy in (
                pltpu.make_async_copy(
                    out_weight_rows.at[k, :, :, pl.ds(0, width)], h_proj.at[k, :, 0], isem.at[2 + 3 * k]
                ),
                pltpu.make_async_copy(
                    out_weight_rows.at[k, :, :, pl.ds(width, width)], h_proj.at[k, :, 1], isem.at[3 + 3 * k]
                ),
            )
        ]
        for copy in loads:
            copy.start()

    def project_out_back(i):
        at = band(i, half)
        att[at, :] = dot_nt(normed[at, :], rows_of(h_out[...])).astype(bf16)

    each(2, project_out_back)

    for copy in fetch:
        copy.wait()

    def attend_back(j, e):
        at = band(e, seq)
        counted = counted_keys(seq, prefix)
        queries = qkv[j, at, :quad]
        all_keys = head_keys(e, j, 1)
        g_out = att[at, j * quad : (j + 1) * quad]
        scores = dot_nt(spread_heads(all_keys), queries)
        g_probs = dot_nt(spread_heads(head_keys(e, j, 2)), g_out)
        low, g_low = [], []
        for h in range(QUAD_HEADS):
            score = scores[h * keys : (h + 1) * keys]
            probs = jnp.exp(jnp.where(counted, score - lse[j, e, h : h + 1, :], MASKED))
            g_prob = g_probs[h * keys : (h + 1) * keys]
            inner = jnp.sum(probs * g_prob, axis=0, keepdims=True)
            low.append(probs.astype(bf16))
            g_low.append((probs * (g_prob - inner)).astype(bf16))
        low = jnp.concatenate(low, axis=0)
        g_low = jnp.concatenate(g_low, axis=0)
        g_queries = from_keys(all_keys, g_low).astype(bf16).T
        g_keys = join_heads(dot_nn(g_low, queries), keys)
        g_values = join_heads(dot_nn(low, g_out), keys)
        qkv[j, at, :quad] = g_queries * HEAD_DIM**-0.5
        qkv[j, at, quad : 2 * quad] = g_keys[:seq].astype(bf16)
        qkv[j, at, 2 * quad :] = g_values[:seq].astype(bf16)
        at = band(e, PAD)
        kept = prefix_grad.dtype
        prefix_grad[at, j * quad : (j + 1) * quad] = g_keys[seq:].astype(kept)
        prefix_grad[at, width + j * quad : width + (j + 1) * quad] = g_values[seq:].astype(kept)

    block_rows = group * PAD

    def total_at(j, h):
        return gacc.at[pl.ds((2 * j + h) * block_rows, block_rows), pl.ds(0, quad)]

    def piece_at(p):
        return gacc.at[pl.ds(p * block_rows, block_rows), pl.ds(quad, quad)]

    def hop(source, target, at, device):
        return pltpu.make_async_remote_copy(
            src_ref=source,
            dst_ref=target,
            send_sem=es_sem.at[at],
            recv_sem=er_sem.at[at],
            device_id=device,
            device_id_type=pl.DeviceIdType.MESH,
        )

    hops = (tasks - 1) + 1 + (line - 1) + 1

    def to_task(j, k):
        return hop(h_tab.at[k, j], from_tasks.at[j, k - 1], j * hops + k - 1, (t ^ k, b))

    def to_core(j):
        mate = (t, place["z"] * 2 + 1 - place["c"])
        return hop(normed.at[pl.ds(j * 2 * block_rows, block_rows), pl.ds(0, quad)], from_core.at[j], j * hops + tasks - 1, mate)

    def to_line(j, k):
        mate = (t, lax.rem(place["z"] + k, line) * 2 + place["c"])
        source = normed.at[pl.ds((2 * j + 1) * block_rows, block_rows), pl.ds(0, quad)]
        return hop(source, from_line.at[j, k - 1], j * hops + tasks - 1 + k, mate)

    def to_half(j):
        mate = (t, place["z"] * 2 + 1 - place["c"])
        return hop(total_at(j, 0), from_half.at[j], j * hops + hops - 1, mate)

    def exchange(j, step):
        if step == 0:
            for h in range(2):
                start = h * width + j * quad
                totals = dot_nn(chosen[...], prefix_grad[:, start : start + quad])
                total_at(j, h)[...] = totals[:block_rows]
                for k in range(1, tasks):
                    h_tab[k, j, h] = (
                        totals[k * block_rows : (k + 1) * block_rows]
                        .astype(bf16)
                        .reshape(group, PAD, quad)
                    )
            for k in range(1, tasks):
                to_task(j, k).start()
        elif step == 1:
            for k in range(1, tasks):
                to_task(j, k).wait_recv()
            sums = []
            for h in range(2):
                total = total_at(j, h)[...]
                for k in range(1, tasks):
                    total = total + from_tasks[j, k - 1, h].astype(f32).reshape(block_rows, quad)
                sums.append(total)
            first = place["c"] == 0
            total_at(j, 0)[...] = jnp.where(first, sums[0], sums[1])
            normed[2 * j * block_rows : (2 * j + 1) * block_rows, :quad] = jnp.where(
                first, sums[1], sums[0]
            ).astype(bf16)
            to_core(j).start()
        elif step == 2:
            to_core(j).wait_recv()
            total = total_at(j, 0)[...] + from_core[j].astype(f32)
            total_at(j, 0)[...] = total
            normed[(2 * j + 1) * block_rows : (2 * j + 2) * block_rows, :quad] = total.astype(bf16)
            for k in range(1, line):
                to_line(j, k).start()
        elif step == 3:
            total = total_at(j, 0)[...]
            for k in range(1, line):
                to_line(j, k).wait_recv()
                total = total + from_line[j, k - 1].astype(f32)
            total_at(j, 0)[...] = total
            to_half(j).start()
        elif step == 4:
            to_half(j).wait_recv()
            own, other = total_at(j, 0)[...], from_half[j]
            first = place["c"] == 0
            piece_at(j)[...] = jnp.where(first, own, other)
            piece_at(QUADS + j)[...] = jnp.where(first, other, own)

    def exchange_tick(now):
        if remote:
            for step in range(4, -1, -1):
                if 0 <= now - step < QUADS:
                    exchange(now - step, step)

    for j in range(QUADS):
        each(examples, functools.partial(attend_back, j))
        exchange_tick(j)

    for n in range(2):
        for i in range(2):
            at = pl.ds(i * half, half)
            to = pl.ds(n * (width // 2), width // 2)
            lead = h_q[0].shape[0]
            parts = [
                dot_nt(
                    qkv[j, at, :],
                    rows_of(h_q[j][n * (lead // 2) : (n + 1) * (lead // 2)])
                    if remote
                    else h_q[j][0, 0, 0, n * (width // 2) : (n + 1) * (width // 2)],
                )
                for j in range(QUADS)
            ]
            acc[at, to] = (parts[0] + parts[1]) + (parts[2] + parts[3])
            if 1 <= 2 * n + i <= 2:
                exchange_tick(QUADS + 2 * n + i - 1)

    fetch_tok.wait()

    def first_norm_back(e):
        at = band(e, seq)
        grad = res[at, :] + norm_back(tok[at, :].astype(f32), gain1[...], acc[at, :])
        tok[at, :] = grad.astype(bf16)

    each(examples // 2, first_norm_back)
    exchange_tick(QUADS + 2)
    each(examples // 2, lambda e: first_norm_back(e + examples // 2))
    exchange_tick(QUADS + 3)
    store_grad = pltpu.make_async_copy(tok, grad_to, isem.at[1])
    store_grad.start()

    if remote:
        for j in range(QUADS):
            for k in range(1, tasks):
                to_task(j, k).wait_send()
            to_core(j).wait_send()
            for k in range(1, line):
                to_line(j, k).wait_send()
            to_half(j).wait_send()
        for copy in loads:
            copy.wait()
        pieces = [piece_at(p)[...] for p in range(2 * QUADS)]
        zeros = jnp.zeros((128 - block_rows, width), bf16)
        table_of = [
            jnp.concatenate(
                [jnp.concatenate(pieces[h * QUADS : (h + 1) * QUADS], axis=1).astype(bf16), zeros],
                axis=0,
            )
            for h in range(2)
        ]
        lane = lax.broadcasted_iota(jnp.int32, (1, 128), 1) // PAD
        flat = jnp.zeros((inner, 128), f32)
        for m in range(group):
            both = dot_nt(rows_of(h_proj[m, :, 0]), table_of[0]) + dot_nt(
                rows_of(h_proj[m, :, 1]), table_of[1]
            )
            flat = jnp.where(lane == m, both, flat)
        act = hid[...]
        g_pre = flat.T * (1.0 - act * act)
        g_low = g_pre.astype(bf16)
        table_to[0], table_to[1] = table_of
        g_pre_to[...] = g_low
        own_hid_to[...] = flat_hid[pl.ds(pl.multiple_of(b * own_inner, 8), own_inner), :]
        embed_to[...] = jnp.concatenate(
            [padded[k, :, pl.ds(pl.multiple_of(b * in_rows, 128), in_rows)] for k in range(group)]
            + [jnp.zeros((128 - block_rows, in_rows), bf16)],
            axis=0,
        ).T
        for m in range(group):
            own_piece = gacc[pl.ds(pl.multiple_of(b * block_rows + m * PAD, 8), PAD), quad : quad + share]
            bias_to[m : m + 1, :] = jnp.sum(own_piece, axis=0, keepdims=True)
            summed = jnp.sum(g_pre[m * PAD : (m + 1) * PAD], axis=0, keepdims=True)
            back = lax.rem(inner - b * own_inner, inner)
            turned = pltpu.roll(jnp.broadcast_to(summed, (8, inner)), back, 1)
            in_bias_to[m : m + 1, :] = turned[:1, :own_inner]
    store_block.wait()
    store_grad.wait()


def run_block(cfg, tokens, cotangent, task_ids, norms, weights, rest):
    rows, width, hidden = cfg["seq"] * cfg["examples"], cfg["width"], cfg["hidden"]
    remote, line, tasks, group = cfg["remote"], cfg["line"], cfg["task"], cfg["group"]
    lead = (tasks, line, 2) if remote else (1, 1, 1)
    shard = lambda w, columns: pltpu.VMEM(lead + (w.shape[0], columns), bf16)
    quad = width // QUADS
    whole = pl.BlockSpec(memory_space=pltpu.VMEM)
    hbm = pl.BlockSpec(memory_space=pl.ANY)
    wide = jax.ShapeDtypeStruct((rows, width), bf16)
    prefix_grad = (cfg["examples"] * PAD, 2 * width)
    if remote:
        share, inner = 2 * width // (2 * line), rest[1].shape[2]
        held = [pltpu.VMEM(lead + (group, PAD, share), bf16)]
        proj = pltpu.VMEM(lead + weights[3].shape, bf16)
        rest = rest + (
            rest[3].reshape(group, line, inner // line, 2 * width),
        )
        rest_specs = [whole, hbm, whole, hbm, whole, hbm]
        outs = [
            wide,
            wide,
            jax.ShapeDtypeStruct((2, 128, width), bf16),
            jax.ShapeDtypeStruct((128, inner), bf16),
            jax.ShapeDtypeStruct((inner // (2 * line), 128), f32),
            jax.ShapeDtypeStruct((width // (2 * line), 128), bf16),
            jax.ShapeDtypeStruct((group, share), f32),
            jax.ShapeDtypeStruct((group, inner // (2 * line)), f32),
        ]
        out_specs = [hbm, hbm] + [whole] * 6
        hops = QUADS * (tasks + line)
        more = [
            pltpu.VMEM(prefix_grad, bf16),
            pltpu.VMEM((tasks * group * PAD, cfg["examples"] * PAD), bf16),
            pltpu.VMEM((group, PAD, width), bf16),
            pltpu.VMEM((128, inner), f32),
            pltpu.VMEM((inner, 128), f32),
            pltpu.VMEM((QUADS, tasks - 1, 2, group, PAD, quad), bf16),
            pltpu.VMEM((QUADS, group * PAD, quad), bf16),
            pltpu.VMEM((QUADS, line - 1, group * PAD, quad), bf16),
            pltpu.VMEM((QUADS, group * PAD, quad), f32),
            pltpu.SemaphoreType.DMA((hops,)),
            pltpu.SemaphoreType.DMA((hops,)),
        ]
    else:
        held = [pltpu.VMEM(rest[0].shape, bf16)]
        proj = pltpu.VMEM((1, CHUNKS, 1, hidden // CHUNKS, width), bf16)
        rest_specs = [hbm]
        outs = [wide, wide, jax.ShapeDtypeStruct(prefix_grad, f32)]
        out_specs = [hbm, hbm, whole]
        more = []
    outs.append(jax.ShapeDtypeStruct((QUADS, rows, 2 * quad), bf16))
    out_specs.append(hbm)
    held += [shard(weights[0], 3 * quad)] * QUADS + [shard(weights[1], width)]
    held += [shard(weights[2], hidden // (2 * CHUNKS))] * (2 * CHUNKS) + [proj]
    count = len(UNITS) * GatherPlane.semaphores(line)
    count = count if remote else 1
    return pl.pallas_call(
        functools.partial(block_kernel, cfg),
        out_shape=outs,
        in_specs=[hbm, hbm, pl.BlockSpec(memory_space=pltpu.SMEM)]
        + [whole] * 4
        + [hbm] * 4
        + rest_specs,
        out_specs=out_specs,
        scratch_shapes=held
        + [
            pltpu.VMEM((rows, width), bf16),
            pltpu.VMEM((rows, width), bf16),
            pltpu.VMEM((QUADS, rows, 3 * quad), bf16),
            pltpu.VMEM((rows, width), bf16),
            pltpu.VMEM((rows, width), bf16),
            pltpu.VMEM((rows, width), f32),
            pltpu.VMEM((rows, width), f32),
            pltpu.VMEM((rows, width), f32),
            pltpu.VMEM((cfg["examples"], PAD, 2 * width), bf16),
            pltpu.VMEM((QUADS, cfg["examples"], QUAD_HEADS, cfg["seq"]), f32),
            pltpu.SemaphoreType.DMA((count,)),
            pltpu.SemaphoreType.DMA((count,)),
            pltpu.SemaphoreType.DMA((128,)),
            pltpu.SemaphoreType.DMA((2 + 3 * group,)),
            pltpu.SemaphoreType.DMA((QUADS + 1,)),
        ]
        + more,
        compiler_params=pltpu.CompilerParams(
            collective_id=0 if remote else None,
            has_side_effects=True,
            vmem_limit_bytes=63 * MIB,
        ),
        name="block",
    )(
        tokens.reshape(rows, width),
        cotangent.reshape(rows, width),
        task_ids,
        *[norm.reshape(1, width) for norm in norms],
        *weights,
        *rest,
    )


def task_kernel(cfg, *refs):
    block_in, grad_in, table, g_pre, own_hid, embed, bias, in_bias, in_weight = refs[:9]
    block_to, grad_to, embed_to, in_to, in_bias_to, out_to, bias_to = refs[9:16]
    own_weight, block_here, grad_here, sems = refs[16:]
    group, width, prefix = cfg["group"], cfg["width"], cfg["prefix"]
    parts = 4
    size = block_in.shape[0] // parts
    own = lax.axis_index("batch")
    copies = []
    for m in range(group):
        copies.append(
            pltpu.make_async_copy(
                in_weight.at[m, pl.ds(pl.multiple_of(own * embed.shape[0], 16), embed.shape[0])],
                own_weight.at[m],
                sems.at[2 * parts + m],
            )
        )
    for i in range(parts):
        at = pl.ds(i * size, size)
        for n, (source, here) in enumerate(((block_in, block_here), (grad_in, grad_here))):
            copies.append(pltpu.make_async_copy(source.at[at], here.at[at], sems.at[2 * i + n]))
    for copy in copies:
        copy.start()
    stores = []
    for i in range(parts):
        at = pl.ds(i * size, size)
        for n, (here, target) in enumerate(((block_here, block_to), (grad_here, grad_to))):
            copies[group + 2 * i + n].wait()
            stores.append(pltpu.make_async_copy(here.at[at], target.at[at], sems.at[2 * i + n]))
            stores[-1].start()
    lane = lax.broadcasted_iota(jnp.int32, (1, 128), 1) // PAD
    for m in range(group):
        left = jnp.where(lane == m, own_hid[...], 0.0).astype(bf16)
        for h in range(2):
            out_to[m, :, h * width : (h + 1) * width] = dot_nn(left, table[h])
        left = jnp.where(lane == m, embed[...].astype(f32), 0.0).astype(bf16)
        in_to[m] = dot_nn(left, g_pre[...])
    in_bias_to[...] = in_bias[...]
    bias_to[...] = bias[...]
    for m in range(group):
        copies[m].wait()
        embed_to[m] = dot_nt(g_pre[m * PAD : (m + 1) * PAD], own_weight[m])[:prefix]
    for copy in stores:
        copy.wait()


def finish_task(cfg, made, in_weight):
    group, inner, width = cfg["group"], in_weight.shape[2], cfg["width"]
    whole = pl.BlockSpec(memory_space=pltpu.VMEM)
    hbm = pl.BlockSpec(memory_space=pl.ANY)
    share = width // (2 * cfg["line"])
    own_inner = inner // (2 * cfg["line"])
    return pl.pallas_call(
        functools.partial(task_kernel, cfg),
        out_shape=(
            jax.ShapeDtypeStruct(made[0].shape, bf16),
            jax.ShapeDtypeStruct(made[1].shape, bf16),
            jax.ShapeDtypeStruct((group, cfg["prefix"], share), f32),
            jax.ShapeDtypeStruct((group, share, inner), f32),
            jax.ShapeDtypeStruct((group, own_inner), f32),
            jax.ShapeDtypeStruct((group, own_inner, 2 * width), f32),
            jax.ShapeDtypeStruct((group, 2 * share), f32),
        ),
        in_specs=[hbm, hbm] + [whole] * 6 + [hbm],
        out_specs=(hbm, hbm) + (whole,) * 5,
        scratch_shapes=[
            pltpu.VMEM((group, share, inner), bf16),
            pltpu.VMEM(made[0].shape, bf16),
            pltpu.VMEM(made[1].shape, bf16),
            pltpu.SemaphoreType.DMA((8 + group,)),
        ],
        compiler_params=pltpu.CompilerParams(vmem_limit_bytes=60 * MIB),
        name="task",
    )(*made, in_weight)


def shards(
    tokens,
    cotangent,
    task_ids,
    qkv_weight,
    out_weight,
    fc_weight,
    proj_weight,
    norm1_gain,
    norm1_shift,
    norm2_gain,
    norm2_shift,
    prefix_embed,
    reparam_in,
    reparam_in_bias,
    reparam_out,
    reparam_out_bias,
):
    group_count, batch = lax.axis_size("task"), lax.axis_size("batch")
    task_group, prefix_len, model_width = prefix_embed.shape
    ex_count, seq_len, _ = tokens.shape
    inner = reparam_in.shape[2]
    slot_count = group_count * CAP
    at_batch = lax.axis_index("batch")
    columns = 2 * model_width // batch
    ff_width = fc_weight.shape[1]
    remote = (
        all(w.shape[0] % 16 == 0 for w in (qkv_weight, out_weight, fc_weight, proj_weight))
        and columns == model_width // QUADS
        and (group_count, batch // 2, task_group) == (4, CHUNKS, QUADS)
        and (2 * inner, ff_width) == (model_width, CHUNKS * model_width)
    )
    weights = (qkv_weight, out_weight, fc_weight, proj_weight)
    norms = (norm1_gain, norm1_shift, norm2_gain, norm2_shift)
    cfg = {
        "seq": seq_len,
        "width": model_width,
        "examples": ex_count,
        "prefix": prefix_len,
        "hidden": ff_width,
        "task": group_count,
        "line": batch // 2,
        "group": task_group,
        "remote": remote,
    }
    if remote:
        rest = (prefix_embed, reparam_in, reparam_in_bias, reparam_out, reparam_out_bias)
        *made, _ = run_block(cfg, tokens, cotangent, task_ids, norms, weights, rest)
        block_out, input_grad, *grads = finish_task(cfg, made, reparam_in)
        return block_out.reshape(tokens.shape), input_grad.reshape(tokens.shape), *grads

    pre_act = (
        jnp.einsum("tpd,tdr->tpr", prefix_embed, reparam_in, preferred_element_type=f32)
        + reparam_in_bias.astype(f32)[:, None, :]
    )
    hidden_act = jnp.tanh(pre_act)
    hidden_low = hidden_act.astype(bf16)
    out_part = lax.dynamic_slice_in_dim(reparam_out, at_batch * columns, columns, 2)
    bias_part = lax.dynamic_slice_in_dim(reparam_out_bias, at_batch * columns, columns, 1)
    table = (
        jnp.einsum("tpr,trc->tpc", hidden_low, out_part, preferred_element_type=f32)
        + bias_part.astype(f32)[:, None, :]
    ).astype(bf16)
    table = jnp.pad(table, ((0, 0), (0, PAD - prefix_len), (0, 0)))
    weights = tuple(lax.all_gather(w, ("task", "batch"), axis=0, tiled=True) for w in weights)
    table = lax.all_gather(
        lax.all_gather(table, "batch", axis=2, tiled=True), "task", axis=0
    )[:, None, None]
    block_out, input_grad, grad_prefix, _ = run_block(
        cfg, tokens, cotangent, task_ids, norms, weights, (table,)
    )
    grad_prefix = grad_prefix.reshape(ex_count, PAD, -1)[:, :prefix_len].reshape(ex_count, -1)

    owners = task_ids // task_group
    local_task = task_ids % task_group
    before = jnp.arange(ex_count)[None, :] < jnp.arange(ex_count)[:, None]
    earlier = jnp.sum((before & (owners[None, :] == owners[:, None])).astype(jnp.int32), axis=1)
    slot_of = owners * CAP + earlier
    slot_hot = slot_of[:, None] == jnp.arange(slot_count)[None, :]
    request = jnp.sum(jnp.where(slot_hot, local_task[:, None] + 1, 0), axis=0) - 1
    received = lax.all_to_all(
        request.reshape(group_count, CAP), "task", split_axis=0, concat_axis=0, tiled=True
    )
    grad_slots = jnp.sum(
        jnp.where(slot_hot[:, :, None], grad_prefix[:, None, :], 0.0), axis=0
    ).astype(bf16)
    incoming = lax.all_to_all(
        grad_slots.reshape(group_count, CAP, -1), "task", split_axis=0, concat_axis=0, tiled=True
    ).astype(f32)
    pick_hot = received.reshape(slot_count)[:, None] == jnp.arange(task_group)[None, :]
    grad_table = jnp.sum(
        jnp.where(pick_hot[:, :, None], incoming.reshape(slot_count, 1, -1), 0.0), axis=0
    )
    grad_table = lax.psum(grad_table, "batch").reshape(task_group, prefix_len, 2 * model_width)

    mine = lambda value, axis: lax.dynamic_slice_in_dim(
        value, at_batch * (value.shape[axis] // batch), value.shape[axis] // batch, axis
    )
    grad_hidden = jnp.einsum(
        "tpc,trc->tpr", grad_table, reparam_out.astype(f32), precision=highest
    )
    grad_pre = grad_hidden * (1.0 - hidden_act * hidden_act)
    grad_out_weight = jnp.einsum(
        "tpr,tpc->trc", mine(hidden_low, 2).astype(f32), grad_table, precision=highest
    )
    grad_out_bias = jnp.sum(mine(grad_table, 2), axis=1)
    grad_in_weight = jnp.einsum(
        "tpd,tpr->tdr", mine(prefix_embed, 2).astype(f32), grad_pre, precision=highest
    )
    grad_in_bias = jnp.sum(mine(grad_pre, 2), axis=1)
    grad_embed = jnp.einsum(
        "tpr,tdr->tpd", grad_pre, mine(reparam_in, 1).astype(f32), precision=highest
    )
    return (
        block_out.reshape(tokens.shape),
        input_grad.reshape(tokens.shape),
        grad_embed,
        grad_in_weight,
        grad_in_bias,
        grad_out_weight,
        grad_out_bias,
    )


def solution(mesh):
    everyone = ("task", "batch")
    return jax.shard_map(
        shards,
        mesh=mesh,
        in_specs=(
            P(everyone, None, None),
            P(everyone, None, None),
            P(everyone),
            P(everyone, None),
            P(everyone, None),
            P(everyone, None),
            P(everyone, None),
            P(),
            P(),
            P(),
            P(),
            P("task", None, None),
            P("task", None, None),
            P("task", None),
            P("task", None, None),
            P("task", None),
        ),
        out_specs=(
            P(everyone, None, None),
            P(everyone, None, None),
            P("task", None, "batch"),
            P("task", "batch", None),
            P("task", "batch"),
            P("task", "batch", None),
            P("task", "batch"),
        ),
        check_vma=False,
    )
```

```python
import functools

import jax
import jax.numpy as jnp
from jax import lax
from jax.experimental import pallas as pl
from jax.experimental.pallas import tpu as pltpu
from jax.sharding import PartitionSpec as P

HEADS = 16
HEAD_DIM = 64
CAP = 2
QUADS = 4
QUAD_HEADS = HEADS // QUADS
PAD = 16
CHUNKS = 4
MASKED = -1e30
MIB = 1024 * 1024

UNITS = ["tab", "q0", "q1", "q2", "q3", "out"] + [f"fc{i}" for i in range(2 * CHUNKS)]
UNITS += [f"p{i}" for i in range(CHUNKS)]
PLACES = {"tab": 1.2, "q0": 0, "q1": 1, "q2": 2, "q3": 3, "out": 4, "p0": 5, "p1": 6, "p2": 7, "p3": 8}
PLACES.update({f"fc{i}": 9 + i for i in range(2 * CHUNKS)})
BY_PLANE = ("q0", "out", "p0", "p2")
LINE_LAGS = (0, 1, 2, 3, 4)
PLANE_LAGS = (0, 1, 2, 3, 4, 5, 6)

highest = lax.Precision.HIGHEST
epsilon = 1e-05
bf16 = jnp.bfloat16
f32 = jnp.float32
NT_DIMS = (((1,), (1,)), ((), ()))


def dot_nn(left, right):
    return jnp.dot(left, right, preferred_element_type=f32)


def dot_nt(left, right):
    return lax.dot_general(left, right, NT_DIMS, preferred_element_type=f32)


def rows_of(value):
    return value.reshape(-1, value.shape[-1])


class Gather:
    def __init__(self, place, held, ssem, rsem, osem, base, owns, window=(0, None)):
        self.place, self.held = place, held
        self.low, self.high = window[0], window[1] or held.shape[3]
        self.ssem, self.rsem, self.osem, self.base = ssem, rsem, osem, base
        self.owns = owns
        self.line = place["line"]
        self.cut = self.line // 2

    @staticmethod
    def semaphores(line):
        return (line - 1) + 8

    def remote(self, ref, at, target):
        return pltpu.make_async_remote_copy(
            src_ref=ref,
            dst_ref=ref,
            send_sem=self.ssem.at[self.base + at],
            recv_sem=self.rsem.at[self.base + at],
            device_id=target,
            device_id_type=pl.DeviceIdType.MESH,
        )

    def own_copies(self):
        slot = self.held.at[self.place["t"], self.place["z"], self.place["c"]]
        return [
            pltpu.make_async_copy(source, slot.at[where], self.osem.at[index])
            for source, where, index in self.owns
        ]

    def to_line(self, k):
        p = self.place
        target = (p["t"], lax.rem(p["z"] + k, self.line) * 2 + p["c"])
        return self.remote(self.held.at[p["t"], p["z"], p["c"], self.low : self.high], k - 1, target)

    def part(self, flip, first, last, at, target):
        p = self.place
        return self.remote(
            self.held.at[p["t"] ^ flip, first:last, p["c"], self.low : self.high],
            self.line - 1 + at,
            target,
        )

    LAGS = LINE_LAGS
    NAMES = ("x", "y", "xr", "yr", "s0", "s1", "s2", "s3")

    def copy(self, name):
        p, n = self.place, self.line
        at = self.NAMES.index(name)
        if name[0] == "s":
            return self.part(int(name[1]), 0, n, at, (p["t"], p["z"] * 2 + 1 - p["c"]))
        step = 1 if name[0] == "x" else 2
        target = (p["t"] ^ step, p["z"] * 2 + p["c"])
        if name[1:] == "r":
            first, last = (0, self.cut) if step == 1 else (self.cut, n)
            return self.part(3 - step, first, last, at, target)
        return self.part(0, 0, n, at, target)

    def begin(self):
        for copy in self.own_copies():
            copy.start()

    def stage(self, step):
        c = self.copy
        if step == 0:
            for copy in self.own_copies():
                copy.wait()
            for k in range(1, self.line):
                self.to_line(k).start()
        elif step == 1:
            for k in range(1, self.line):
                self.to_line(k).wait_recv()
            c("x").start()
            c("y").start()
            c("s0").start()
        elif step == 2:
            c("x").wait_recv()
            c("yr").start()
            c("s1").start()
            c("y").wait_recv()
            c("xr").start()
            c("s2").start()
        elif step == 3:
            c("xr").wait_recv()
            c("yr").wait_recv()
            c("s3").start()
        elif step == 4:
            for name in ("s0", "s1", "s2", "s3"):
                c(name).wait_recv()

    def finish(self):
        for k in range(1, self.line):
            self.to_line(k).wait_send()
        for name in self.NAMES:
            self.copy(name).wait_send()


class GatherPlane(Gather):
    LAGS = PLANE_LAGS

    @staticmethod
    def semaphores(line):
        return 4 + 2 * (line - 1) + line

    def mate(self, z, c=None):
        p = self.place
        return (p["t"], lax.rem(z + self.line, self.line) * 2 + (p["c"] if c is None else c))

    def plane(self, z, at, target):
        return self.remote(
            self.held.at[
                :, lax.rem(z + self.line, self.line), self.place["c"], self.low : self.high
            ],
            at,
            target,
        )

    def part(self, flip, low, high, at, target):
        p = self.place
        return self.remote(self.held.at[p["t"] ^ flip, p["z"], p["c"], low:high], at, target)

    def copy(self, name):
        p = self.place
        half = (self.low + self.high) // 2
        step = 1 if name[0] == "x" else 2
        target = (p["t"] ^ step, p["z"] * 2 + p["c"])
        if name[1:] == "r":
            low, high = (self.low, half) if step == 1 else (half, self.high)
            return self.part(3 - step, low, high, 1 + step, target)
        return self.part(0, self.low, self.high, step - 1, target)

    def up(self, k):
        return self.plane(self.place["z"] - (k - 1), 3 + k, self.mate(self.place["z"] + 1))

    def down(self, k):
        return self.plane(
            self.place["z"] + (k - 1), 2 + self.line + k, self.mate(self.place["z"] - 1)
        )

    def from_below(self, k):
        return self.plane(self.place["z"] - k, 3 + k, self.mate(self.place["z"] + 1))

    def from_above(self, k):
        return self.plane(
            self.place["z"] + k, 2 + self.line + k, self.mate(self.place["z"] - 1)
        )

    def across(self, z):
        mate = self.mate(self.place["z"], 1 - self.place["c"])
        return self.plane(z, 4 + 2 * (self.line - 1) + z, mate)

    def stage(self, step):
        c, z, last = self.copy, self.place["z"], self.line - 1
        if step == 0:
            for copy in self.own_copies():
                copy.wait()
            c("x").start()
            c("y").start()
        elif step == 1:
            c("x").wait_recv()
            c("yr").start()
            c("y").wait_recv()
            c("xr").start()
        elif step == 2:
            c("xr").wait_recv()
            c("yr").wait_recv()
            pl.when(z < last)(lambda: self.up(1).start())
            pl.when(z > 0)(lambda: self.down(1).start())
            self.across(z).start()
        elif step < 3 + last:
            k = step - 2

            @pl.when(z >= k)
            def _():
                self.from_below(k).wait_recv()
                if k < last:
                    pl.when(z < last)(lambda: self.up(k + 1).start())
                self.across(z - k).start()

            @pl.when(z + k <= last)
            def _():
                self.from_above(k).wait_recv()
                if k < last:
                    pl.when(z > 0)(lambda: self.down(k + 1).start())
                self.across(z + k).start()

        elif step == 3 + last:
            for other in range(self.line):
                self.across(other).wait_recv()

    def finish(self):
        z, last = self.place["z"], self.line - 1
        for name in ("x", "y", "xr", "yr"):
            self.copy(name).wait_send()
        for k in range(1, self.line):
            pl.when((z < last) & (z >= k - 1))(lambda k=k: self.up(k).wait_send())
            pl.when((z > 0) & (z + k - 1 <= last))(lambda k=k: self.down(k).wait_send())
        for other in range(self.line):
            self.across(other).wait_send()


class Local:
    LAGS = LINE_LAGS

    def __init__(self, held, osem, owns):
        self.held, self.osem, self.owns = held, osem, owns

    def own_copies(self):
        return [
            pltpu.make_async_copy(source, self.held.at[where], self.osem.at[index])
            for source, where, index in self.owns
        ]

    def begin(self):
        for copy in self.own_copies():
            copy.start()

    def stage(self, step):
        if step == 4:
            for copy in self.own_copies():
                copy.wait()

    def finish(self):
        pass


class Pump:
    def __init__(self, units, places):
        self.units = units
        keyed = [
            (places[u] + lag, step, u)
            for u in range(len(units))
            for step, lag in enumerate(units[u].LAGS)
        ]
        self.order = [(u, step) for _, step, u in sorted(keyed)]
        self.done = 0

    def begin(self):
        for unit in self.units:
            unit.begin()

    def run(self, count):
        for _ in range(count):
            if self.done < len(self.order):
                u, step = self.order[self.done]
                self.units[u].stage(step)
                self.done += 1

    def ready(self, unit):
        last = self.order.index((unit, len(self.units[unit].LAGS) - 1)) + 1
        self.run(max(0, last - self.done))

    def finish(self):
        self.run(len(self.order))
        for unit in self.units:
            unit.finish()


def norm_parts(value):
    average = jnp.mean(value, -1, keepdims=True)
    centred = value - average
    spread = jnp.mean(centred * centred, -1, keepdims=True)
    inverse = lax.rsqrt(spread + epsilon)
    return centred * inverse, inverse


def norm_back(value, gain, grad):
    hat, inverse = norm_parts(value)
    scaled = grad * gain
    first = jnp.mean(scaled, -1, keepdims=True)
    second = jnp.mean(scaled * hat, -1, keepdims=True)
    return inverse * (scaled - first - hat * second)


def spread_heads(block):
    lane = lax.broadcasted_iota(jnp.int32, (1, block.shape[1]), 1) // HEAD_DIM
    return jnp.concatenate(
        [jnp.where(lane == h, block, jnp.zeros_like(block)) for h in range(QUAD_HEADS)], axis=0
    )


def join_heads(block, rows):
    lane = lax.broadcasted_iota(jnp.int32, (1, block.shape[1]), 1) // HEAD_DIM
    total = block[:rows]
    for h in range(1, QUAD_HEADS):
        total = jnp.where(lane == h, block[h * rows : (h + 1) * rows], total)
    return total


def counted_keys(seq, prefix):
    key = lax.broadcasted_iota(jnp.int32, (seq + PAD, seq), 0)
    query = lax.broadcasted_iota(jnp.int32, (seq + PAD, seq), 1)
    return jnp.where(key < seq, key, jnp.where(key < seq + prefix, 0, seq)) <= query


def block_kernel(cfg, *refs):
    it = iter(refs)
    take = lambda n: [next(it) for _ in range(n)]
    tok_in, cot_in, ids, gain1, shift1, gain2, shift2 = take(7)
    wqkv, wout, wfc, wproj = take(4)
    remote = cfg["remote"]
    if remote:
        embed, in_weight, in_bias, out_weight, out_bias = take(5)
        (out_weight_rows,) = take(1)
        block_to, grad_to, table_to, g_pre_to, own_hid_to, embed_to, bias_to, in_bias_to, kept = take(9)
    else:
        (table,) = take(1)
        block_to, grad_to, prefix_grad, kept = take(4)
    h_tab, h_q0, h_q1, h_q2, h_q3, h_out = take(6)
    h_fc = take(2 * CHUNKS)
    (h_proj,) = take(1)
    tok, cot, qkv, normed, att, res, acc, gacc, pkv, lse = take(10)
    ssem, rsem, osem, isem = take(4)
    keep_sem = take(1)[0]
    if remote:
        prefix_grad, chosen, padded, hid, flat_hid, from_tasks, from_core, from_line, from_half = take(9)
        es_sem, er_sem = take(2)
    h_q = (h_q0, h_q1, h_q2, h_q3)

    seq, width, examples, prefix = cfg["seq"], cfg["width"], cfg["examples"], cfg["prefix"]
    rows, hidden, line = seq * examples, cfg["hidden"], cfg["line"]
    tasks, group = cfg["task"], cfg["group"]
    quad = width // QUADS
    keys = seq + PAD

    load_tok = pltpu.make_async_copy(tok_in, tok, isem.at[0])
    load_cot = pltpu.make_async_copy(cot_in, cot, isem.at[1])
    load_tok.start()
    load_cot.start()
    if remote:
        t, b = lax.axis_index("task"), lax.axis_index("batch")
        place = {"t": t, "z": b // 2, "c": lax.rem(b, 2), "line": line}
        inner = in_weight.shape[2]
        own_inner, in_rows = inner // (2 * line), width // (2 * line)
        share = 2 * width // (2 * line)
        loads = [
            copy
            for k in range(group)
            for copy in (
                pltpu.make_async_copy(
                    in_weight.at[k], qkv.at[k, :, pl.ds(0, inner)], isem.at[2 + 2 * k]
                ),
                pltpu.make_async_copy(
                    out_weight.at[k, :, pl.ds(pl.multiple_of(b * share, 128), share)],
                    qkv.at[k, pl.ds(0, inner), pl.ds(inner, share)],
                    isem.at[3 + 2 * k],
                ),
            )
        ]
        for copy in loads:
            copy.start()

    own = iter(range(128))
    cols = lambda start, size: pl.ds(start, size)
    everything = (slice(None),)
    sources = [(h_tab, [] if remote else [(table, everything)])]
    for j in range(QUADS):
        sources.append(
            (
                h_q[j],
                [
                    (wqkv.at[:, cols(part * width + j * quad, quad)], (slice(None), cols(part * quad, quad)))
                    for part in range(3)
                ],
            )
        )
    sources.append((h_out, [(wout, everything)]))
    groups = tasks if remote else 1
    piece = hidden // (2 * CHUNKS)
    some = piece // groups
    fc_at = 2 + QUADS
    for f in range(2 * CHUNKS):
        sources.append(
            (
                h_fc[f],
                [
                    (
                        wfc.at[:, cols((g * 2 * CHUNKS + f) * some, some)],
                        (slice(None), cols(g * some, some)),
                    )
                    for g in range(groups)
                ],
            )
        )
    units = []
    base = 0
    for at, (held, owns) in enumerate(sources):
        if remote:
            kind = GatherPlane if UNITS[at] in BY_PLANE else Gather
            numbered = [(s, w, next(own)) for s, w in owns]
            units.append(kind(place, held, ssem, rsem, osem, base, numbered))
            base += kind.semaphores(line)
        else:
            lead = (0, 0, 0) if at > 0 else ()
            units.append(
                Local(held, osem, [(s, lead + w if at > 0 else w, next(own)) for s, w in owns])
            )
    fc_units = list(range(fc_at, fc_at + len(h_fc)))
    proj_units = []
    for i in range(CHUNKS):
        proj_units.append(len(units))
        if remote:
            size = wproj.shape[0] // CHUNKS
            at = pl.ds(i * size, size)
            numbered = [(wproj.at[at], (at,), next(own))]
            window = (i * size, (i + 1) * size)
            units.append(Gather(place, h_proj, ssem, rsem, osem, base, numbered, window))
            base += Gather.semaphores(line)
        else:
            size = hidden // CHUNKS
            units.append(
                Local(h_proj, osem, [(wproj.at[pl.ds(i * size, size)], (0, i, 0), next(own))])
            )
    places = [PLACES[n] for n in UNITS]
    pump = Pump(units, places)
    pump.begin()
    if remote:
        barrier = pltpu.get_barrier_semaphore()
        mates = [(t, lax.rem(place["z"] + k, line) * 2 + place["c"]) for k in range(1, line)]
        mates += [(t ^ 1, b), (t ^ 2, b), (t, place["z"] * 2 + 1 - place["c"])]
        for mate in mates:
            pl.semaphore_signal(barrier, inc=1, device_id=mate, device_id_type=pl.DeviceIdType.MESH)
        pl.semaphore_wait(barrier, len(mates))
    pump.run(2)

    def each(count, body):
        lax.fori_loop(0, count, lambda i, carry: (body(i), carry)[1], 0)

    def band(i, size):
        return pl.ds(pl.multiple_of(i * size, size), size)

    if remote:
        for copy in loads:
            copy.wait()
        padded[...] = jnp.zeros_like(padded)
        for k in range(group):
            padded[k, :prefix, :] = embed[k]
        hid[...] = jnp.zeros_like(hid)
        for k in range(group):
            act = jnp.tanh(
                dot_nn(padded[k], qkv[k, :, :inner]) + in_bias[k : k + 1, :].astype(f32)
            )
            hid[k * PAD : (k + 1) * PAD, :] = act
            own_bias = out_bias[:, pl.ds(pl.multiple_of(b * share, 128), share)].astype(f32)
            h_tab[t, place["z"], place["c"], k] = (
                dot_nn(act.astype(bf16), qkv[k, :inner, inner : inner + share])
                + own_bias[k : k + 1, :]
            ).astype(bf16)
        flat_hid[...] = hid[...].T
    load_tok.wait()

    def first_norm(e):
        at = band(e, seq)
        hat, _ = norm_parts(tok[at, :].astype(f32))
        normed[at, :] = (hat * gain1[...] + shift1[...]).astype(bf16)

    each(examples, first_norm)

    pump.ready(0)
    lead = h_tab.shape[:3]
    piece_cols = h_tab.shape[-1]

    for e in range(examples):
        number = ids[e]
        owner, local = number // group, lax.rem(number, group)
        for z in range(lead[1]):
            for c in range(lead[2]):
                where = (z * lead[2] + c) * piece_cols
                pkv[e, :, where : where + piece_cols] = h_tab[owner, z, c, local]

    if remote:
        row = lax.broadcasted_iota(jnp.int32, chosen.shape, 0)
        column = lax.broadcasted_iota(jnp.int32, chosen.shape, 1)
        wanted, given = jnp.full(chosen.shape, -1, jnp.int32), jnp.full(chosen.shape, -2, jnp.int32)
        for k in range(tasks):
            first = k * group * PAD
            number = (t ^ k) * group + (row - first) // PAD
            wanted = jnp.where((row >= first) & (row < first + group * PAD), number, wanted)
        for e in range(examples):
            given = jnp.where(column // PAD == e, ids[e], given)
        met = (wanted == given) & (lax.rem(row, PAD) == lax.rem(column, PAD))
        chosen[...] = met.astype(f32).astype(bf16)

    def head_keys(e, j, part):
        at = band(e, seq)
        return jnp.concatenate(
            [
                qkv[j, at, part * quad : (part + 1) * quad],
                pkv[e, :, (part - 1) * width + j * quad : (part - 1) * width + (j + 1) * quad],
            ],
            axis=0,
        )

    def from_keys(block, weights):
        flipped = block[:seq].T
        heads = [
            dot_nn(
                flipped[h * HEAD_DIM : (h + 1) * HEAD_DIM], weights[h * keys : h * keys + seq]
            )
            for h in range(QUAD_HEADS)
        ]
        extra = spread_heads(block[seq:]).T
        low = jnp.concatenate(
            [weights[h * keys + seq : (h + 1) * keys] for h in range(QUAD_HEADS)], axis=0
        )
        return jnp.concatenate(heads, axis=0) + dot_nn(extra, low)

    def attend(j, e):
        at = band(e, seq)
        counted = counted_keys(seq, prefix)
        scores = dot_nt(spread_heads(head_keys(e, j, 1)), qkv[j, at, :quad])
        weights, inverse = [], []
        for h in range(QUAD_HEADS):
            score = jnp.where(counted, scores[h * keys : (h + 1) * keys], MASKED)
            top = jnp.max(score, axis=0, keepdims=True)
            exps = jnp.exp(score - top)
            total = jnp.sum(exps, axis=0, keepdims=True)
            lse[j, e, h : h + 1, :] = top + jnp.log(total)
            weights.append(exps.astype(bf16))
            inverse.append(jnp.broadcast_to(1.0 / total, (HEAD_DIM, seq)))
        out = from_keys(head_keys(e, j, 2), jnp.concatenate(weights, axis=0))
        out = out * jnp.concatenate(inverse, axis=0)
        att[at, j * quad : (j + 1) * quad] = out.astype(bf16).T

    half = rows // 2
    spill = [
        pltpu.make_async_copy(qkv.at[j, :, pl.ds(0, 2 * quad)], kept.at[j], keep_sem.at[j])
        for j in range(QUADS)
    ]
    fetch = [
        pltpu.make_async_copy(kept.at[j], qkv.at[j, :, pl.ds(0, 2 * quad)], keep_sem.at[j])
        for j in range(QUADS)
    ]
    fetch_tok = pltpu.make_async_copy(tok_in, tok, keep_sem.at[QUADS])
    for j in range(QUADS):
        pump.ready(1 + j)

        def project(i, j=j):
            at = band(i, half)
            mixed = dot_nn(normed[at, :], rows_of(h_q[j][...]))
            qkv[j, at, :quad] = (mixed[:, :quad] * HEAD_DIM**-0.5).astype(bf16)
            qkv[j, at, quad:] = mixed[:, quad:].astype(bf16)

        each(2, project)
        pump.run(2)
        each(examples, functools.partial(attend, j))
        spill[j].start()
        pump.run(2)

    pump.ready(1 + QUADS)

    def project_out(i):
        at = band(i, half)
        res[at, :] = tok[at, :].astype(f32) + dot_nn(att[at, :], rows_of(h_out[...]))

    each(2, project_out)
    pump.run(2)

    def second_norm(e):
        at = band(e, seq)
        hat, _ = norm_parts(res[at, :])
        normed[at, :] = (hat * gain2[...] + shift2[...]).astype(bf16)

    each(examples, second_norm)

    slope = 0.7978845608028654
    cubic = 0.044715 * slope

    load_cot.wait()
    def down_rows(f, at):
        if remote:
            return rows_of(h_proj[:, f // 2, f % 2, :, at])
        return h_proj[0, f // 2, 0, (f % 2) * piece : (f % 2 + 1) * piece, at]

    def g_act_at(f):
        if f % 2 == 0:
            return qkv.at[f // 2, :, pl.ds(0, piece)]
        return (att if f < CHUNKS else tok).at[:, pl.ds((f // 2 % 2) * piece, piece)]

    for copy in spill:
        copy.wait()
    for f in range(2 * CHUNKS):
        if f == 0 or not remote:
            for unit in proj_units:
                pump.ready(unit)

        def back_down(r, f=f):
            at = band(r, half)
            g_act_at(f)[at, :] = dot_nt(cot[at, :], down_rows(f, slice(None))).astype(bf16)

        each(2, back_down)
        pump.run(1)

    for f in range(2 * CHUNKS):
        pump.ready(fc_units[f])
        pump.run(3)

        def feed(r, f=f):
            at = band(r, half)
            up = dot_nn(normed[at, :], rows_of(h_fc[f][...]))
            g_act = g_act_at(f)[at, :].astype(f32)
            square = up * up
            bend = jnp.tanh(up * (slope + cubic * square))
            raised = 0.5 + 0.5 * bend
            active = (up * raised).astype(bf16)
            turn = 0.5 * (1.0 - bend * bend) * (slope + 3.0 * cubic * square)
            g_up = (g_act * (raised + up * turn)).astype(bf16)
            tops = h_fc[f].shape[0] // 2
            for n in range(2):
                to = slice(n * (width // 2), (n + 1) * (width // 2))
                down = dot_nn(active, down_rows(f, to))
                acc[at, to] = down if f == 0 else acc[at, to] + down
            for n in range(2):
                to = slice(n * (width // 2), (n + 1) * (width // 2))
                back = dot_nt(
                    g_up,
                    rows_of(h_fc[f][n * tops : (n + 1) * tops]) if remote else h_fc[f][0, 0, 0, to],
                )
                gacc[at, to] = back if f == 0 else gacc[at, to] + back

        each(2, feed)
    pump.finish()
    for copy in fetch:
        copy.start()
    fetch_tok.start()

    def second_norm_back(e):
        at = band(e, seq)
        value = res[at, :]
        grad = cot[at, :].astype(f32) + norm_back(value, gain2[...], gacc[at, :])
        cot[at, :] = (value + acc[at, :]).astype(bf16)
        res[at, :] = grad
        normed[at, :] = grad.astype(bf16)

    each(examples, second_norm_back)
    store_block = pltpu.make_async_copy(cot, block_to, isem.at[0])
    store_block.start()
    if remote:
        loads = [
            copy
            for k in range(group)
            for copy in (
                pltpu.make_async_copy(
                    out_weight_rows.at[k, :, :, pl.ds(0, width)], h_proj.at[k, :, 0], isem.at[2 + 3 * k]
                ),
                pltpu.make_async_copy(
                    out_weight_rows.at[k, :, :, pl.ds(width, width)], h_proj.at[k, :, 1], isem.at[3 + 3 * k]
                ),
            )
        ]
        for copy in loads:
            copy.start()

    def project_out_back(i):
        at = band(i, half)
        att[at, :] = dot_nt(normed[at, :], rows_of(h_out[...])).astype(bf16)

    each(2, project_out_back)

    for copy in fetch:
        copy.wait()

    def attend_back(j, e):
        at = band(e, seq)
        counted = counted_keys(seq, prefix)
        queries = qkv[j, at, :quad]
        all_keys = head_keys(e, j, 1)
        g_out = att[at, j * quad : (j + 1) * quad]
        scores = dot_nt(spread_heads(all_keys), queries)
        g_probs = dot_nt(spread_heads(head_keys(e, j, 2)), g_out)
        low, g_low = [], []
        for h in range(QUAD_HEADS):
            score = scores[h * keys : (h + 1) * keys]
            probs = jnp.exp(jnp.where(counted, score - lse[j, e, h : h + 1, :], MASKED))
            g_prob = g_probs[h * keys : (h + 1) * keys]
            inner = jnp.sum(probs * g_prob, axis=0, keepdims=True)
            low.append(probs.astype(bf16))
            g_low.append((probs * (g_prob - inner)).astype(bf16))
        low = jnp.concatenate(low, axis=0)
        g_low = jnp.concatenate(g_low, axis=0)
        g_queries = from_keys(all_keys, g_low).astype(bf16).T
        g_keys = join_heads(dot_nn(g_low, queries), keys)
        g_values = join_heads(dot_nn(low, g_out), keys)
        qkv[j, at, :quad] = g_queries * HEAD_DIM**-0.5
        qkv[j, at, quad : 2 * quad] = g_keys[:seq].astype(bf16)
        qkv[j, at, 2 * quad :] = g_values[:seq].astype(bf16)
        at = band(e, PAD)
        kept = prefix_grad.dtype
        prefix_grad[at, j * quad : (j + 1) * quad] = g_keys[seq:].astype(kept)
        prefix_grad[at, width + j * quad : width + (j + 1) * quad] = g_values[seq:].astype(kept)

    block_rows = group * PAD

    def total_at(j, h):
        return gacc.at[pl.ds((2 * j + h) * block_rows, block_rows), pl.ds(0, quad)]

    def piece_at(p):
        return gacc.at[pl.ds(p * block_rows, block_rows), pl.ds(quad, quad)]

    def hop(source, target, at, device):
        return pltpu.make_async_remote_copy(
            src_ref=source,
            dst_ref=target,
            send_sem=es_sem.at[at],
            recv_sem=er_sem.at[at],
            device_id=device,
            device_id_type=pl.DeviceIdType.MESH,
        )

    hops = (tasks - 1) + 1 + (line - 1) + 1

    def to_task(j, k):
        return hop(h_tab.at[k, j], from_tasks.at[j, k - 1], j * hops + k - 1, (t ^ k, b))

    def to_core(j):
        mate = (t, place["z"] * 2 + 1 - place["c"])
        return hop(normed.at[pl.ds(j * 2 * block_rows, block_rows), pl.ds(0, quad)], from_core.at[j], j * hops + tasks - 1, mate)

    def to_line(j, k):
        mate = (t, lax.rem(place["z"] + k, line) * 2 + place["c"])
        source = normed.at[pl.ds((2 * j + 1) * block_rows, block_rows), pl.ds(0, quad)]
        return hop(source, from_line.at[j, k - 1], j * hops + tasks - 1 + k, mate)

    def to_half(j):
        mate = (t, place["z"] * 2 + 1 - place["c"])
        return hop(total_at(j, 0), from_half.at[j], j * hops + hops - 1, mate)

    def exchange(j, step):
        if step == 0:
            for h in range(2):
                start = h * width + j * quad
                totals = dot_nn(chosen[...], prefix_grad[:, start : start + quad])
                total_at(j, h)[...] = totals[:block_rows]
                for k in range(1, tasks):
                    h_tab[k, j, h] = (
                        totals[k * block_rows : (k + 1) * block_rows]
                        .astype(bf16)
                        .reshape(group, PAD, quad)
                    )
            for k in range(1, tasks):
                to_task(j, k).start()
        elif step == 1:
            for k in range(1, tasks):
                to_task(j, k).wait_recv()
            sums = []
            for h in range(2):
                total = total_at(j, h)[...]
                for k in range(1, tasks):
                    total = total + from_tasks[j, k - 1, h].astype(f32).reshape(block_rows, quad)
                sums.append(total)
            first = place["c"] == 0
            total_at(j, 0)[...] = jnp.where(first, sums[0], sums[1])
            normed[2 * j * block_rows : (2 * j + 1) * block_rows, :quad] = jnp.where(
                first, sums[1], sums[0]
            ).astype(bf16)
            to_core(j).start()
        elif step == 2:
            to_core(j).wait_recv()
            total = total_at(j, 0)[...] + from_core[j].astype(f32)
            total_at(j, 0)[...] = total
            normed[(2 * j + 1) * block_rows : (2 * j + 2) * block_rows, :quad] = total.astype(bf16)
            for k in range(1, line):
                to_line(j, k).start()
        elif step == 3:
            total = total_at(j, 0)[...]
            for k in range(1, line):
                to_line(j, k).wait_recv()
                total = total + from_line[j, k - 1].astype(f32)
            total_at(j, 0)[...] = total
            to_half(j).start()
        elif step == 4:
            to_half(j).wait_recv()
            own, other = total_at(j, 0)[...], from_half[j]
            first = place["c"] == 0
            piece_at(j)[...] = jnp.where(first, own, other)
            piece_at(QUADS + j)[...] = jnp.where(first, other, own)

    def exchange_tick(now):
        if remote:
            for step in range(4, -1, -1):
                if 0 <= now - step < QUADS:
                    exchange(now - step, step)

    for j in range(QUADS):
        each(examples, functools.partial(attend_back, j))
        exchange_tick(j)

    for n in range(2):
        for i in range(2):
            at = pl.ds(i * half, half)
            to = pl.ds(n * (width // 2), width // 2)
            lead = h_q[0].shape[0]
            parts = [
                dot_nt(
                    qkv[j, at, :],
                    rows_of(h_q[j][n * (lead // 2) : (n + 1) * (lead // 2)])
                    if remote
                    else h_q[j][0, 0, 0, n * (width // 2) : (n + 1) * (width // 2)],
                )
                for j in range(QUADS)
            ]
            acc[at, to] = (parts[0] + parts[1]) + (parts[2] + parts[3])
            if 1 <= 2 * n + i <= 2:
                exchange_tick(QUADS + 2 * n + i - 1)

    fetch_tok.wait()

    def first_norm_back(e):
        at = band(e, seq)
        grad = res[at, :] + norm_back(tok[at, :].astype(f32), gain1[...], acc[at, :])
        tok[at, :] = grad.astype(bf16)

    each(examples // 2, first_norm_back)
    exchange_tick(QUADS + 2)
    each(examples // 2, lambda e: first_norm_back(e + examples // 2))
    exchange_tick(QUADS + 3)
    store_grad = pltpu.make_async_copy(tok, grad_to, isem.at[1])
    store_grad.start()

    if remote:
        for j in range(QUADS):
            for k in range(1, tasks):
                to_task(j, k).wait_send()
            to_core(j).wait_send()
            for k in range(1, line):
                to_line(j, k).wait_send()
            to_half(j).wait_send()
        for copy in loads:
            copy.wait()
        pieces = [piece_at(p)[...] for p in range(2 * QUADS)]
        zeros = jnp.zeros((128 - block_rows, width), bf16)
        table_of = [
            jnp.concatenate(
                [jnp.concatenate(pieces[h * QUADS : (h + 1) * QUADS], axis=1).astype(bf16), zeros],
                axis=0,
            )
            for h in range(2)
        ]
        lane = lax.broadcasted_iota(jnp.int32, (1, 128), 1) // PAD
        flat = jnp.zeros((inner, 128), f32)
        for m in range(group):
            both = dot_nt(rows_of(h_proj[m, :, 0]), table_of[0]) + dot_nt(
                rows_of(h_proj[m, :, 1]), table_of[1]
            )
            flat = jnp.where(lane == m, both, flat)
        act = hid[...]
        g_pre = flat.T * (1.0 - act * act)
        g_low = g_pre.astype(bf16)
        table_to[0], table_to[1] = table_of
        g_pre_to[...] = g_low
        own_hid_to[...] = flat_hid[pl.ds(pl.multiple_of(b * own_inner, 8), own_inner), :]
        embed_to[...] = jnp.concatenate(
            [padded[k, :, pl.ds(pl.multiple_of(b * in_rows, 128), in_rows)] for k in range(group)]
            + [jnp.zeros((128 - block_rows, in_rows), bf16)],
            axis=0,
        ).T
        for m in range(group):
            own_piece = gacc[pl.ds(pl.multiple_of(b * block_rows + m * PAD, 8), PAD), quad : quad + share]
            bias_to[m : m + 1, :] = jnp.sum(own_piece, axis=0, keepdims=True)
            summed = jnp.sum(g_pre[m * PAD : (m + 1) * PAD], axis=0, keepdims=True)
            back = lax.rem(inner - b * own_inner, inner)
            turned = pltpu.roll(jnp.broadcast_to(summed, (8, inner)), back, 1)
            in_bias_to[m : m + 1, :] = turned[:1, :own_inner]
    store_block.wait()
    store_grad.wait()


def run_block(cfg, tokens, cotangent, task_ids, norms, weights, rest):
    rows, width, hidden = cfg["seq"] * cfg["examples"], cfg["width"], cfg["hidden"]
    remote, line, tasks, group = cfg["remote"], cfg["line"], cfg["task"], cfg["group"]
    lead = (tasks, line, 2) if remote else (1, 1, 1)
    shard = lambda w, columns: pltpu.VMEM(lead + (w.shape[0], columns), bf16)
    quad = width // QUADS
    whole = pl.BlockSpec(memory_space=pltpu.VMEM)
    hbm = pl.BlockSpec(memory_space=pl.ANY)
    wide = jax.ShapeDtypeStruct((rows, width), bf16)
    prefix_grad = (cfg["examples"] * PAD, 2 * width)
    if remote:
        share, inner = 2 * width // (2 * line), rest[1].shape[2]
        held = [pltpu.VMEM(lead + (group, PAD, share), bf16)]
        proj = pltpu.VMEM(lead + weights[3].shape, bf16)
        rest = rest + (
            rest[3].reshape(group, line, inner // line, 2 * width),
        )
        rest_specs = [whole, hbm, whole, hbm, whole, hbm]
        outs = [
            wide,
            wide,
            jax.ShapeDtypeStruct((2, 128, width), bf16),
            jax.ShapeDtypeStruct((128, inner), bf16),
            jax.ShapeDtypeStruct((inner // (2 * line), 128), f32),
            jax.ShapeDtypeStruct((width // (2 * line), 128), bf16),
            jax.ShapeDtypeStruct((group, share), f32),
            jax.ShapeDtypeStruct((group, inner // (2 * line)), f32),
        ]
        out_specs = [hbm, hbm] + [whole] * 6
        hops = QUADS * (tasks + line)
        more = [
            pltpu.VMEM(prefix_grad, bf16),
            pltpu.VMEM((tasks * group * PAD, cfg["examples"] * PAD), bf16),
            pltpu.VMEM((group, PAD, width), bf16),
            pltpu.VMEM((128, inner), f32),
            pltpu.VMEM((inner, 128), f32),
            pltpu.VMEM((QUADS, tasks - 1, 2, group, PAD, quad), bf16),
            pltpu.VMEM((QUADS, group * PAD, quad), bf16),
            pltpu.VMEM((QUADS, line - 1, group * PAD, quad), bf16),
            pltpu.VMEM((QUADS, group * PAD, quad), f32),
            pltpu.SemaphoreType.DMA((hops,)),
            pltpu.SemaphoreType.DMA((hops,)),
        ]
    else:
        held = [pltpu.VMEM(rest[0].shape, bf16)]
        proj = pltpu.VMEM((1, CHUNKS, 1, hidden // CHUNKS, width), bf16)
        rest_specs = [hbm]
        outs = [wide, wide, jax.ShapeDtypeStruct(prefix_grad, f32)]
        out_specs = [hbm, hbm, whole]
        more = []
    outs.append(jax.ShapeDtypeStruct((QUADS, rows, 2 * quad), bf16))
    out_specs.append(hbm)
    held += [shard(weights[0], 3 * quad)] * QUADS + [shard(weights[1], width)]
    held += [shard(weights[2], hidden // (2 * CHUNKS))] * (2 * CHUNKS) + [proj]
    count = len(UNITS) * GatherPlane.semaphores(line)
    count = count if remote else 1
    return pl.pallas_call(
        functools.partial(block_kernel, cfg),
        out_shape=outs,
        in_specs=[hbm, hbm, pl.BlockSpec(memory_space=pltpu.SMEM)]
        + [whole] * 4
        + [hbm] * 4
        + rest_specs,
        out_specs=out_specs,
        scratch_shapes=held
        + [
            pltpu.VMEM((rows, width), bf16),
            pltpu.VMEM((rows, width), bf16),
            pltpu.VMEM((QUADS, rows, 3 * quad), bf16),
            pltpu.VMEM((rows, width), bf16),
            pltpu.VMEM((rows, width), bf16),
            pltpu.VMEM((rows, width), f32),
            pltpu.VMEM((rows, width), f32),
            pltpu.VMEM((rows, width), f32),
            pltpu.VMEM((cfg["examples"], PAD, 2 * width), bf16),
            pltpu.VMEM((QUADS, cfg["examples"], QUAD_HEADS, cfg["seq"]), f32),
            pltpu.SemaphoreType.DMA((count,)),
            pltpu.SemaphoreType.DMA((count,)),
            pltpu.SemaphoreType.DMA((128,)),
            pltpu.SemaphoreType.DMA((2 + 3 * group,)),
            pltpu.SemaphoreType.DMA((QUADS + 1,)),
        ]
        + more,
        compiler_params=pltpu.CompilerParams(
            collective_id=0 if remote else None,
            has_side_effects=True,
            vmem_limit_bytes=63 * MIB,
        ),
        name="block",
    )(
        tokens.reshape(rows, width),
        cotangent.reshape(rows, width),
        task_ids,
        *[norm.reshape(1, width) for norm in norms],
        *weights,
        *rest,
    )


def task_kernel(cfg, *refs):
    block_in, grad_in, table, g_pre, own_hid, embed, bias, in_bias, in_weight = refs[:9]
    block_to, grad_to, embed_to, in_to, in_bias_to, out_to, bias_to = refs[9:16]
    own_weight, block_here, grad_here, sems = refs[16:]
    group, width, prefix = cfg["group"], cfg["width"], cfg["prefix"]
    parts = 4
    size = block_in.shape[0] // parts
    own = lax.axis_index("batch")
    copies = []
    for m in range(group):
        copies.append(
            pltpu.make_async_copy(
                in_weight.at[m, pl.ds(pl.multiple_of(own * embed.shape[0], 16), embed.shape[0])],
                own_weight.at[m],
                sems.at[2 * parts + m],
            )
        )
    for i in range(parts):
        at = pl.ds(i * size, size)
        for n, (source, here) in enumerate(((block_in, block_here), (grad_in, grad_here))):
            copies.append(pltpu.make_async_copy(source.at[at], here.at[at], sems.at[2 * i + n]))
    for copy in copies:
        copy.start()
    stores = []

    def hand_on(i):
        at = pl.ds(i * size, size)
        for n, (here, target) in enumerate(((block_here, block_to), (grad_here, grad_to))):
            copies[group + 2 * i + n].wait()
            stores.append(pltpu.make_async_copy(here.at[at], target.at[at], sems.at[2 * i + n]))
            stores[-1].start()

    lane = lax.broadcasted_iota(jnp.int32, (1, 128), 1) // PAD
    for m in range(group):
        left = jnp.where(lane == m, own_hid[...], 0.0).astype(bf16)
        for h in range(2):
            out_to[m, :, h * width : (h + 1) * width] = dot_nn(left, table[h])
        left = jnp.where(lane == m, embed[...].astype(f32), 0.0).astype(bf16)
        in_to[m] = dot_nn(left, g_pre[...])
        if m < parts:
            hand_on(m)
    for i in range(group, parts):
        hand_on(i)
    in_bias_to[...] = in_bias[...]
    bias_to[...] = bias[...]
    for m in range(group):
        copies[m].wait()
        embed_to[m] = dot_nt(g_pre[m * PAD : (m + 1) * PAD], own_weight[m])[:prefix]
    for copy in stores:
        copy.wait()


def finish_task(cfg, made, in_weight):
    group, inner, width = cfg["group"], in_weight.shape[2], cfg["width"]
    whole = pl.BlockSpec(memory_space=pltpu.VMEM)
    hbm = pl.BlockSpec(memory_space=pl.ANY)
    share = width // (2 * cfg["line"])
    own_inner = inner // (2 * cfg["line"])
    return pl.pallas_call(
        functools.partial(task_kernel, cfg),
        out_shape=(
            jax.ShapeDtypeStruct(made[0].shape, bf16),
            jax.ShapeDtypeStruct(made[1].shape, bf16),
            jax.ShapeDtypeStruct((group, cfg["prefix"], share), f32),
            jax.ShapeDtypeStruct((group, share, inner), f32),
            jax.ShapeDtypeStruct((group, own_inner), f32),
            jax.ShapeDtypeStruct((group, own_inner, 2 * width), f32),
            jax.ShapeDtypeStruct((group, 2 * share), f32),
        ),
        in_specs=[hbm, hbm] + [whole] * 6 + [hbm],
        out_specs=(hbm, hbm) + (whole,) * 5,
        scratch_shapes=[
            pltpu.VMEM((group, share, inner), bf16),
            pltpu.VMEM(made[0].shape, bf16),
            pltpu.VMEM(made[1].shape, bf16),
            pltpu.SemaphoreType.DMA((8 + group,)),
        ],
        compiler_params=pltpu.CompilerParams(vmem_limit_bytes=60 * MIB),
        name="task",
    )(*made, in_weight)


def shards(
    tokens,
    cotangent,
    task_ids,
    qkv_weight,
    out_weight,
    fc_weight,
    proj_weight,
    norm1_gain,
    norm1_shift,
    norm2_gain,
    norm2_shift,
    prefix_embed,
    reparam_in,
    reparam_in_bias,
    reparam_out,
    reparam_out_bias,
):
    group_count, batch = lax.axis_size("task"), lax.axis_size("batch")
    task_group, prefix_len, model_width = prefix_embed.shape
    ex_count, seq_len, _ = tokens.shape
    inner = reparam_in.shape[2]
    slot_count = group_count * CAP
    at_batch = lax.axis_index("batch")
    columns = 2 * model_width // batch
    ff_width = fc_weight.shape[1]
    remote = (
        all(w.shape[0] % 16 == 0 for w in (qkv_weight, out_weight, fc_weight, proj_weight))
        and columns == model_width // QUADS
        and (group_count, batch // 2, task_group) == (4, CHUNKS, QUADS)
        and (2 * inner, ff_width) == (model_width, CHUNKS * model_width)
    )
    weights = (qkv_weight, out_weight, fc_weight, proj_weight)
    norms = (norm1_gain, norm1_shift, norm2_gain, norm2_shift)
    cfg = {
        "seq": seq_len,
        "width": model_width,
        "examples": ex_count,
        "prefix": prefix_len,
        "hidden": ff_width,
        "task": group_count,
        "line": batch // 2,
        "group": task_group,
        "remote": remote,
    }
    if remote:
        rest = (prefix_embed, reparam_in, reparam_in_bias, reparam_out, reparam_out_bias)
        *made, _ = run_block(cfg, tokens, cotangent, task_ids, norms, weights, rest)
        block_out, input_grad, *grads = finish_task(cfg, made, reparam_in)
        return block_out.reshape(tokens.shape), input_grad.reshape(tokens.shape), *grads

    pre_act = (
        jnp.einsum("tpd,tdr->tpr", prefix_embed, reparam_in, preferred_element_type=f32)
        + reparam_in_bias.astype(f32)[:, None, :]
    )
    hidden_act = jnp.tanh(pre_act)
    hidden_low = hidden_act.astype(bf16)
    out_part = lax.dynamic_slice_in_dim(reparam_out, at_batch * columns, columns, 2)
    bias_part = lax.dynamic_slice_in_dim(reparam_out_bias, at_batch * columns, columns, 1)
    table = (
        jnp.einsum("tpr,trc->tpc", hidden_low, out_part, preferred_element_type=f32)
        + bias_part.astype(f32)[:, None, :]
    ).astype(bf16)
    table = jnp.pad(table, ((0, 0), (0, PAD - prefix_len), (0, 0)))
    weights = tuple(lax.all_gather(w, ("task", "batch"), axis=0, tiled=True) for w in weights)
    table = lax.all_gather(
        lax.all_gather(table, "batch", axis=2, tiled=True), "task", axis=0
    )[:, None, None]
    block_out, input_grad, grad_prefix, _ = run_block(
        cfg, tokens, cotangent, task_ids, norms, weights, (table,)
    )
    grad_prefix = grad_prefix.reshape(ex_count, PAD, -1)[:, :prefix_len].reshape(ex_count, -1)

    owners = task_ids // task_group
    local_task = task_ids % task_group
    before = jnp.arange(ex_count)[None, :] < jnp.arange(ex_count)[:, None]
    earlier = jnp.sum((before & (owners[None, :] == owners[:, None])).astype(jnp.int32), axis=1)
    slot_of = owners * CAP + earlier
    slot_hot = slot_of[:, None] == jnp.arange(slot_count)[None, :]
    request = jnp.sum(jnp.where(slot_hot, local_task[:, None] + 1, 0), axis=0) - 1
    received = lax.all_to_all(
        request.reshape(group_count, CAP), "task", split_axis=0, concat_axis=0, tiled=True
    )
    grad_slots = jnp.sum(
        jnp.where(slot_hot[:, :, None], grad_prefix[:, None, :], 0.0), axis=0
    ).astype(bf16)
    incoming = lax.all_to_all(
        grad_slots.reshape(group_count, CAP, -1), "task", split_axis=0, concat_axis=0, tiled=True
    ).astype(f32)
    pick_hot = received.reshape(slot_count)[:, None] == jnp.arange(task_group)[None, :]
    grad_table = jnp.sum(
        jnp.where(pick_hot[:, :, None], incoming.reshape(slot_count, 1, -1), 0.0), axis=0
    )
    grad_table = lax.psum(grad_table, "batch").reshape(task_group, prefix_len, 2 * model_width)

    mine = lambda value, axis: lax.dynamic_slice_in_dim(
        value, at_batch * (value.shape[axis] // batch), value.shape[axis] // batch, axis
    )
    grad_hidden = jnp.einsum(
        "tpc,trc->tpr", grad_table, reparam_out.astype(f32), precision=highest
    )
    grad_pre = grad_hidden * (1.0 - hidden_act * hidden_act)
    grad_out_weight = jnp.einsum(
        "tpr,tpc->trc", mine(hidden_low, 2).astype(f32), grad_table, precision=highest
    )
    grad_out_bias = jnp.sum(mine(grad_table, 2), axis=1)
    grad_in_weight = jnp.einsum(
        "tpd,tpr->tdr", mine(prefix_embed, 2).astype(f32), grad_pre, precision=highest
    )
    grad_in_bias = jnp.sum(mine(grad_pre, 2), axis=1)
    grad_embed = jnp.einsum(
        "tpr,tdr->tpd", grad_pre, mine(reparam_in, 1).astype(f32), precision=highest
    )
    return (
        block_out.reshape(tokens.shape),
        input_grad.reshape(tokens.shape),
        grad_embed,
        grad_in_weight,
        grad_in_bias,
        grad_out_weight,
        grad_out_bias,
    )


def solution(mesh):
    everyone = ("task", "batch")
    return jax.shard_map(
        shards,
        mesh=mesh,
        in_specs=(
            P(everyone, None, None),
            P(everyone, None, None),
            P(everyone),
            P(everyone, None),
            P(everyone, None),
            P(everyone, None),
            P(everyone, None),
            P(),
            P(),
            P(),
            P(),
            P("task", None, None),
            P("task", None, None),
            P("task", None),
            P("task", None, None),
            P("task", None),
        ),
        out_specs=(
            P(everyone, None, None),
            P(everyone, None, None),
            P("task", None, "batch"),
            P("task", "batch", None),
            P("task", "batch"),
            P("task", "batch", None),
            P("task", "batch"),
        ),
        check_vma=False,
    )
```
